256 devices in a mesh: dp: 4 (over x), tm: 16 (over z, core), head: 4 (over y).
Axes of the slice: x: 4, y: 4, z: 8, core: 2. Of those that a mesh axis runs over, the one named last changes fastest.
Arguments:
- query_in: bfloat16 [4, 1024, 1280], P('dp', 'tm'), may hold values from -60 to 60
- grad_out: bfloat16 [4, 1024, 1280], P('dp', 'tm'), may hold values from -6 to 6
- encoder_states: bfloat16 [4, 4096, 1280], P('dp', 'tm'), may hold values from -24 to 24
- frame_lengths: int32 [4], P('dp'), may hold values from 2048 to 4096, as said below
- w_query: bfloat16 [1280, 1280], P(None, 'head'), may hold values from -0.15625 to 0.15625
- w_key: bfloat16 [1280, 1280], P(None, 'head'), may hold values from -0.15625 to 0.15625
- w_value: bfloat16 [1280, 1280], P(None, 'head'), may hold values from -0.15625 to 0.15625
- w_out: bfloat16 [1280, 1280], P('head'), may hold values from -0.15625 to 0.15625
Outputs:
- grad_query_in: bfloat16 [4, 1024, 1280], P('dp', 'tm', 'head')
- grad_encoder: bfloat16 [4, 4096, 1280], P('dp', 'tm', 'head')
- grad_w_query: float32 [1280, 1280], P(('dp', 'tm'), 'head')
- grad_w_key: float32 [1280, 1280], P(('dp', 'tm'), 'head')
- grad_w_value: float32 [1280, 1280], P(('dp', 'tm'), 'head')
- grad_w_out: float32 [1280, 1280], P('head', ('dp', 'tm'))
The draws below stay inside these ranges and needn't reach their ends.
Inputs may be any that keep to these rules, and one draw needn't show every extreme that they name: `frame_lengths`: multiples of 128; some recording has all 4096 frames valid and another exactly half of them.
All inputs are finite; a program needn't handle non-finite values.
Results may differ from the reference program's by a relative error of at most 0.024.
The reference program's roundings to bfloat16 on the way (of `query`, `dout`, `dscores` and `dquery`) count: a program that leaves them out, or rounds other values in their place, can miss the bound.
Values may be sent and summed in bfloat16 or wider, within the bound.
No kernel may reach another device: no remote copies, remote signals or barrier semaphores. Data moves between devices by JAX's collectives and lax.ppermute only.
A program may use at most 128 MiB of HBM per device.

```python
import jax
import jax.numpy as jnp
from jax import lax

D = 1280
HD = 64
HEADS = 20
FRAMES = 4096
Q = 1024
REC = 4


def draw_query_in(key, part):
    key = jax.random.fold_in(key, 11)
    first = jax.random.fold_in(key, 0)
    base = jnp.clip(jax.random.normal(first, (REC, Q, D), jnp.float32), -6.0, 6.0)
    return base.astype(jnp.bfloat16)


def draw_encoder_states(key, part):
    key = jax.random.fold_in(key, 23)
    first = jax.random.fold_in(key, 0)
    base = jnp.clip(jax.random.normal(first, (REC, FRAMES, D), jnp.float32), -6.0, 6.0)
    return base.astype(jnp.bfloat16)


def draw_frame_lengths(key, part):
    key = jax.random.fold_in(key, 37)
    first, second = jax.random.split(key)
    slab_count = FRAMES // 128
    drawn = jax.random.randint(first, (REC,), slab_count // 2, slab_count + 1) * 128
    order = jax.random.permutation(second, REC)
    rank = jnp.argsort(order).astype(jnp.int32)
    drawn = jnp.where(rank == 0, FRAMES, drawn)
    drawn = jnp.where(rank == 1, slab_count // 2 * 128, drawn)
    return drawn.astype(jnp.int32)


def block_scale(rng, shape, cuts, least, high):
    factor_of, own = 1.0, jax.random.fold_in(rng, 6)
    for dim, shards_of in cuts:
        draws = jnp.exp(jax.random.uniform(jax.random.fold_in(own, dim), (shards_of,), jnp.float32, least / len(cuts), high / len(cuts)))
        factor_of = factor_of * jnp.repeat(draws, shape[dim] // shards_of).reshape([-1 if axis == dim else 1 for axis in range(len(shape))])
    return factor_of


def noise(rng, extent, spread, reach, shards=(), kind=jnp.bfloat16):
    level = block_scale(rng, extent, shards, -0.22, 0.18) if shards else 1.0
    entries = jax.random.normal(rng, extent, jnp.float32) * spread * level
    return jnp.minimum(jnp.maximum(entries, -reach), reach).astype(kind)


def setup_inputs(seed: int = 0) -> dict:
    key_list = jax.random.split(jax.random.key(seed), 9)
    query_in = draw_query_in(jax.random.fold_in(key_list[8], 71), 0)
    grad_out = noise(key_list[1], (REC, Q, D), 1.0, 6.0, ((0, 4), (1, 16)))
    encoder_states = draw_encoder_states(jax.random.fold_in(key_list[8], 71), 0)
    frame_lengths = draw_frame_lengths(jax.random.fold_in(key_list[8], 71), 0)
    w_query = noise(key_list[4], (D, HEADS * HD), D ** -0.5, 0.15625, ((1, 4),))
    w_key = noise(key_list[5], (D, HEADS * HD), D ** -0.5, 0.15625, ((1, 4),))
    w_value = noise(key_list[6], (D, HEADS * HD), D ** -0.5, 0.15625, ((1, 4),))
    w_out = noise(key_list[7], (HEADS * HD, D), (HEADS * HD) ** -0.5, 0.15625, ((0, 4),))
    return {"query_in": query_in, "grad_out": grad_out, "encoder_states": encoder_states, "frame_lengths": frame_lengths, "w_query": w_query, "w_key": w_key, "w_value": w_value, "w_out": w_out}


def head_terms(frame_mask, operands):
    query_head, key_head, value_head, dout_head = operands
    score_scale = HD ** -0.5
    scores = jnp.dot(query_head, key_head.T, preferred_element_type=jnp.float32) * score_scale
    scores = jnp.where(frame_mask[None, :], scores, -1e30)
    row_top = jnp.max(scores, axis=1, keepdims=True)
    weights_exp = jnp.where(frame_mask[None, :], jnp.exp(scores - row_top), 0.0)
    row_sum = jnp.sum(weights_exp, axis=1, keepdims=True)
    probs = weights_exp / row_sum
    attended = jnp.dot(probs, value_head.astype(jnp.float32), precision=lax.Precision.HIGHEST)
    row_delta = jnp.sum(dout_head.astype(jnp.float32) * attended, axis=1, keepdims=True)
    dprobs = jnp.dot(dout_head, value_head.T, preferred_element_type=jnp.float32)
    dscores = (probs * (dprobs - row_delta)).astype(jnp.bfloat16)
    dquery = jnp.dot(dscores, key_head, preferred_element_type=jnp.float32) * score_scale
    dkey = (jnp.dot(dscores.T, query_head, preferred_element_type=jnp.float32) * score_scale).astype(jnp.bfloat16)
    dvalue = jnp.dot(probs.astype(jnp.bfloat16).T, dout_head, preferred_element_type=jnp.float32).astype(jnp.bfloat16)
    return attended, dquery, dkey, dvalue


def split_heads(matrix):
    return jnp.transpose(matrix.reshape(matrix.shape[0], HEADS, HD), (1, 0, 2))


def join_heads(stacked):
    return jnp.transpose(stacked, (1, 0, 2)).reshape(stacked.shape[1], HEADS * HD)


def reference(query_in, grad_out, encoder_states, frame_lengths, w_query, w_key, w_value, w_out):
    grad_inputs = []
    grad_frames = []
    total_q = jnp.zeros((D, HEADS * HD), jnp.float32)
    total_k = jnp.zeros((D, HEADS * HD), jnp.float32)
    total_v = jnp.zeros((D, HEADS * HD), jnp.float32)
    total_o = jnp.zeros((HEADS * HD, D), jnp.float32)
    for record in range(REC):
        rows_in = query_in[record]
        rows_grad = grad_out[record]
        frames = encoder_states[record]
        query = jnp.dot(rows_in, w_query, preferred_element_type=jnp.float32).astype(jnp.bfloat16)
        keys = jnp.dot(frames, w_key, preferred_element_type=jnp.float32).astype(jnp.bfloat16)
        values = jnp.dot(frames, w_value, preferred_element_type=jnp.float32).astype(jnp.bfloat16)
        dout = jnp.dot(rows_grad, w_out.T, preferred_element_type=jnp.float32).astype(jnp.bfloat16)
        frame_mask = jnp.arange(FRAMES, dtype=jnp.int32) < frame_lengths[record]
        attended, dquery, dkey, dvalue = lax.map(
            lambda operands: head_terms(frame_mask, operands),
            (split_heads(query), split_heads(keys), split_heads(values), split_heads(dout)))
        attended = join_heads(attended)
        dquery = join_heads(dquery).astype(jnp.bfloat16)
        dkey = join_heads(dkey)
        dvalue = join_heads(dvalue)
        grad_inputs.append(jnp.dot(dquery, w_query.T, preferred_element_type=jnp.float32).astype(jnp.bfloat16))
        frame_term = jnp.dot(dkey, w_key.T, preferred_element_type=jnp.float32) + jnp.dot(dvalue, w_value.T, preferred_element_type=jnp.float32)
        grad_frames.append(frame_term.astype(jnp.bfloat16))
        total_q = total_q + jnp.dot(rows_in.T, dquery, preferred_element_type=jnp.float32)
        total_k = total_k + jnp.dot(frames.T, dkey, preferred_element_type=jnp.float32)
        total_v = total_v + jnp.dot(frames.T, dvalue, preferred_element_type=jnp.float32)
        total_o = total_o + jnp.dot(attended.astype(jnp.bfloat16).T, rows_grad, preferred_element_type=jnp.float32)
    return jnp.stack(grad_inputs), jnp.stack(grad_frames), total_q, total_k, total_v, total_o
```

```python
import functools
import math

import jax
import jax.numpy as jnp
from jax import lax
from jax.experimental import pallas as pl
from jax.experimental.pallas import tpu as pltpu
from jax.sharding import Mesh, PartitionSpec as P

HD = 64
BF = jnp.bfloat16
F32 = jnp.float32
SCALE = HD ** (-0.5)
LOG2 = SCALE * math.log2(math.e)
LOW = -1e30
NT = (((1,), (1,)), ((), ()))
TN = (((0,), (0,)), ((), ()))


def mm(left, right, dims=None):
    if dims is None:
        dims = (((1,), (0,)), ((), ()))
    return lax.dot_general(left, right, dims, preferred_element_type=F32)


def ring(x, axis, size, step):
    return lax.ppermute(x, axis, [(i, (i + step) % size) for i in range(size)])


def swap(x, axis):
    return lax.ppermute(x, axis, [(0, 1), (1, 0)])


def frame_bias(valid_ref, block, rows):
    positions = lax.broadcasted_iota(jnp.int32, (rows, 1), 0)
    return jnp.where(positions < valid_ref[block], 0.0, LOW)


def stats_kernel(heads, valid_ref, *refs):
    rows_refs, frame_refs, out_ref = refs[:4], refs[4:8], refs[8]
    width = heads * HD
    rows = jnp.concatenate([r[...] for r in rows_refs], axis=0)
    blocks = [r[...] for r in frame_refs]
    biases = [frame_bias(valid_ref, j, b.shape[0]) for j, b in enumerate(blocks)]
    out_ref[...] = jnp.zeros_like(out_ref)
    for h in range(heads):
        cut = slice(h * HD, (h + 1) * HD)
        cut2 = slice(width + h * HD, width + (h + 1) * HD)
        query, dout = rows[:, cut], rows[:, cut2]
        scores = [
            mm(b[:, cut], query, NT) * LOG2 + bias for b, bias in zip(blocks, biases)
        ]
        top = functools.reduce(
            jnp.maximum, [jnp.max(s, axis=0, keepdims=True) for s in scores]
        )
        top = jnp.maximum(top, 0.1 * LOW)
        total = jnp.zeros_like(top)
        delta = jnp.zeros_like(top)
        for s, b in zip(scores, blocks):
            weight = jnp.exp2(s - top)
            dprobs = mm(b[:, cut2], dout, NT)
            total += jnp.sum(weight, axis=0, keepdims=True)
            delta += jnp.sum(weight * dprobs, axis=0, keepdims=True)
        total = jnp.maximum(total, 1.0)
        out_ref[h : h + 1, :] = top + jnp.log2(total)
        out_ref[8 + h : 9 + h, :] = delta / total


def grads_kernel(heads, valid_ref, *refs):
    rows_refs, frame_refs, stat_refs = refs[:4], refs[4:8], refs[8:12]
    keep_ref, send_ref = refs[12:14]
    dq_refs = refs[14:18]
    width = heads * HD
    rows = jnp.concatenate([r[...] for r in rows_refs], axis=0)
    blocks = [r[...] for r in frame_refs]
    part = blocks[0].shape[0]
    own = rows_refs[0].shape[0]
    stats = [stat_refs[0][...]] + [
        pltpu.roll(stat_refs[k][...], own * k, 1) for k in (1, 2, 3)
    ]
    tops = [s[:8] for s in stats]
    top = functools.reduce(jnp.maximum, tops)
    shares = [jnp.exp2(t - top) for t in tops]
    total = functools.reduce(jnp.add, shares)
    lse = top + jnp.log2(total)
    delta = functools.reduce(
        jnp.add, [w * s[8:] for w, s in zip(shares, stats)]
    ) / total
    biases = [frame_bias(valid_ref, j, part) for j in range(4)]
    dq_t, att_t = [], []
    for h in range(heads):
        cut = slice(h * HD, (h + 1) * HD)
        cut2 = slice(width + h * HD, width + (h + 1) * HD)
        query, dout = rows[:, cut], rows[:, cut2]
        dq_sum = jnp.zeros((HD, rows.shape[0]), F32)
        att_sum = jnp.zeros((HD, rows.shape[0]), F32)
        for j, (b, bias) in enumerate(zip(blocks, biases)):
            key, value = b[:, cut], b[:, cut2]
            scores = mm(key, query, NT) * LOG2 + bias
            probs = jnp.exp2(scores - lse[h : h + 1])
            dprobs = mm(value, dout, NT)
            dscores = (probs * (dprobs - delta[h : h + 1])).astype(BF)
            probs = probs.astype(BF)
            dkey = mm(dscores, query) * SCALE
            dvalue = mm(probs, dout)
            out_ref = send_ref if j % 2 else keep_ref
            span = slice((j // 2) * part, (j // 2 + 1) * part)
            out_ref[span, cut] = dkey.astype(out_ref.dtype)
            out_ref[span, cut2] = dvalue.astype(out_ref.dtype)
            dq_sum += mm(key, dscores, TN)
            att_sum += mm(value, probs, TN)
        dq_t.append(dq_sum * SCALE)
        att_t.append(att_sum)
    joined = jnp.concatenate(dq_t + att_t, axis=0).T
    for k in range(4):
        dq_refs[k][...] = joined[k * own : (k + 1) * own].astype(dq_refs[k].dtype)


def weights_kernel(part, xt_ref, xt2_ref, y_ref, y2_ref, *out_refs):
    frames = y_ref.shape[0] - part
    half = y_ref.shape[1] // 2
    step = out_refs[0].shape[0]
    pairs = ((xt_ref, y_ref), (xt2_ref, y2_ref))
    for k, out_ref in enumerate(out_refs):
        span = slice(k * step, (k + 1) * step)
        kv = sum(mm(x[span, :frames], y[:frames, :]) for x, y in pairs)
        q = sum(
            mm(x[span, frames : frames + part], y[frames : frames + part, :half])
            for x, y in pairs
        )
        o = sum(
            mm(x[span, frames + part :], y[frames : frames + part, half:])
            for x, y in pairs
        )
        out_ref[:, : 2 * half] = kv.astype(out_ref.dtype)
        out_ref[:, 2 * half : 3 * half] = q.astype(out_ref.dtype)
        out_ref[:, 3 * half :] = o.astype(out_ref.dtype)


VMEM = pl.BlockSpec(memory_space=pltpu.VMEM)
SMEM = pl.BlockSpec(memory_space=pltpu.SMEM)
PARAMS = pltpu.CompilerParams(vmem_limit_bytes=48 * 1024 * 1024)


def per_device(query_in, grad_out, encoder_states, frame_lengths, w_query, w_key, w_value, w_out):
    rows_in, rows_grad, frames = query_in[0], grad_out[0], encoder_states[0]
    width = w_query.shape[1]
    heads = width // HD
    model = w_query.shape[0]
    own, slab = rows_in.shape[0], frames.shape[0]
    xi, ai, bi, ci, yi = (lax.axis_index(n) for n in ("dp", "a", "b", "core", "head"))

    query = mm(rows_in, w_query).astype(BF)
    dout = mm(rows_grad, w_out, NT).astype(BF)
    rows0 = jnp.concatenate([query, dout], axis=1)
    row_blocks = [rows0] + [ring(rows0, "a", 4, j) for j in (1, 2, 3)]

    w_kv = jnp.concatenate([w_key, w_value], axis=1)
    kv = mm(frames, w_kv).astype(BF)
    kv_pair = swap(kv, "b")
    frame_blocks = [kv, swap(kv, "core"), kv_pair, swap(kv_pair, "core")]
    starts = [
        slab * (4 * ai + 2 * (bi ^ db) + (ci ^ dc)) for db in (0, 1) for dc in (0, 1)
    ]
    valid = jnp.stack([frame_lengths[0] - s for s in starts]).astype(jnp.int32)

    place = jnp.arange(model, dtype=jnp.int32)
    inner = model // 64
    rest, unit = place // inner, place % inner
    a_rel, b_rel = rest % 4, (rest // 4) % 2
    x_rel, c_rel = (rest // 8) % 4, rest // 32
    target = (
        ((x_rel + xi) % 4) * 16 + ((a_rel + ai) % 4) * 4 + (b_rel ^ bi) * 2 + (c_rel ^ ci)
    ) * inner + unit
    pick = (place[:, None] == target[None, :]).astype(BF)
    stacked = jnp.concatenate([frames, rows_in, rows_grad], axis=0)
    turned = mm(pick, stacked, (((0,), (1,)), ((), ()))).astype(BF)
    turned_own = turned[: model // 2]
    turned_other = swap(turned[model // 2 :], "core")

    stats = pl.pallas_call(
        functools.partial(stats_kernel, heads),
        out_shape=jax.ShapeDtypeStruct((16, 4 * own), F32),
        in_specs=[SMEM] + [VMEM] * 8,
        out_specs=VMEM,
        compiler_params=PARAMS,
    )(valid, *row_blocks, *frame_blocks)
    all_stats = [stats] + [ring(stats, "a", 4, j) for j in (1, 2, 3)]

    keep, send, dq0, dq1, dq2, dq3 = pl.pallas_call(
        functools.partial(grads_kernel, heads),
        out_shape=[
            jax.ShapeDtypeStruct((2 * slab, 2 * width), F32),
            jax.ShapeDtypeStruct((2 * slab, 2 * width), BF),
            jax.ShapeDtypeStruct((own, 2 * width), F32),
        ]
        + [jax.ShapeDtypeStruct((own, 2 * width), BF)] * 3,
        in_specs=[SMEM] + [VMEM] * 12,
        out_specs=[VMEM] * 6,
        compiler_params=PARAMS,
    )(valid, *row_blocks, *frame_blocks, *all_stats)

    recv = swap(send, "core").astype(F32)
    pair = (keep[slab:] + recv[slab:]).astype(BF)
    pair_recv = swap(pair, "b").astype(F32)
    dq_recv = [ring(d, "a", 4, -j).astype(F32) for j, d in ((1, dq1), (2, dq2), (3, dq3))]
    dkv = (keep[:slab] + recv[:slab] + pair_recv).astype(BF)
    dqo = (dq0 + dq_recv[0] + dq_recv[1] + dq_recv[2]).astype(BF)
    grads = jnp.concatenate([dkv, dqo], axis=0)
    grads_other = swap(grads, "core")

    parts = []
    for k in range(4):
        start = ((yi + k) % 4) * width
        w_kv_rows = lax.dynamic_slice_in_dim(w_kv, start, width, 0)
        w_q_rows = lax.dynamic_slice_in_dim(w_query, start, width, 0)
        parts.append(
            jnp.concatenate(
                [mm(dkv, w_kv_rows, NT), mm(dqo[:, :width], w_q_rows, NT)], axis=0
            ).astype(BF if k else F32)
        )
    arrived = [ring(parts[k], "head", 4, k).astype(F32) for k in (1, 2, 3)]
    inputs = (parts[0] + arrived[0] + arrived[1] + arrived[2]).astype(BF)
    dframes, dinput = inputs[:slab], inputs[slab:]

    step = model // 8
    pieces = pl.pallas_call(
        functools.partial(weights_kernel, own),
        out_shape=[jax.ShapeDtypeStruct((step, 4 * width), F32)]
        + [jax.ShapeDtypeStruct((step, 4 * width), BF)] * 3,
        in_specs=[VMEM] * 4,
        out_specs=[VMEM] * 4,
        compiler_params=PARAMS,
    )(turned_own, turned_other, grads, grads_other)
    over_x = [ring(pieces[k], "dp", 4, k).astype(F32) for k in (1, 2, 3)]
    total = pieces[0] + over_x[0] + over_x[1] + over_x[2]
    total = total[: step // 2] + swap(total[step // 2 :].astype(BF), "b").astype(F32)
    low = total.astype(BF)
    over_a = [
        ring(low[k * inner : (k + 1) * inner], "a", 4, k).astype(F32) for k in (1, 2, 3)
    ]
    total = total[:inner] + over_a[0] + over_a[1] + over_a[2]
    return (
        dinput[None],
        dframes[None],
        total[:, 2 * width : 3 * width],
        total[:, :width],
        total[:, width : 2 * width],
        total[:, 3 * width :].T,
    )


def solution(mesh):
    dp, tm, head = mesh.devices.shape
    fine = Mesh(mesh.devices.reshape(dp, 4, 2, 2, head), ("dp", "a", "b", "core", "head"))
    tm = ("a", "b", "core")
    placed = (
        P("dp", tm, None),
        P("dp", tm, None),
        P("dp", tm, None),
        P("dp"),
        P(None, "head"),
        P(None, "head"),
        P(None, "head"),
        P("head", None),
    )
    every = ("dp",) + tm
    return jax.shard_map(
        per_device,
        mesh=fine,
        in_specs=placed,
        out_specs=(
            P("dp", tm, "head"),
            P("dp", tm, "head"),
            P(every, "head"),
            P(every, "head"),
            P(every, "head"),
            P("head", every),
        ),
        check_vma=False,
    )
```

```python
import functools
import math

import jax
import jax.numpy as jnp
from jax import lax
from jax.experimental import pallas as pl
from jax.experimental.pallas import tpu as pltpu
from jax.sharding import Mesh, PartitionSpec as P

HD = 64
BF = jnp.bfloat16
F32 = jnp.float32
SCALE = HD ** (-0.5)
LOG2 = SCALE * math.log2(math.e)
LOW = -1e30
NT = (((1,), (1,)), ((), ()))
TN = (((0,), (0,)), ((), ()))


def mm(left, right, dims=None):
    if dims is None:
        dims = (((1,), (0,)), ((), ()))
    return lax.dot_general(left, right, dims, preferred_element_type=F32)


def ring(x, axis, size, step):
    return lax.ppermute(x, axis, [(i, (i + step) % size) for i in range(size)])


def swap(x, axis):
    return lax.ppermute(x, axis, [(0, 1), (1, 0)])


def frame_bias(valid_ref, block, rows):
    positions = lax.broadcasted_iota(jnp.int32, (rows, 1), 0)
    return jnp.where(positions < valid_ref[block], 0.0, LOW)


def stats_kernel(heads, valid_ref, *refs):
    rows_refs, frame_refs, out_ref = refs[:4], refs[4:8], refs[8]
    width = heads * HD
    rows = jnp.concatenate([r[...] for r in rows_refs], axis=0)
    blocks = [r[...] for r in frame_refs]
    biases = [frame_bias(valid_ref, j, b.shape[0]) for j, b in enumerate(blocks)]
    out_ref[...] = jnp.zeros_like(out_ref)
    for h in range(heads):
        cut = slice(h * HD, (h + 1) * HD)
        cut2 = slice(width + h * HD, width + (h + 1) * HD)
        query, dout = rows[:, cut], rows[:, cut2]
        scores = [
            mm(b[:, cut], query, NT) * LOG2 + bias for b, bias in zip(blocks, biases)
        ]
        top = functools.reduce(
            jnp.maximum, [jnp.max(s, axis=0, keepdims=True) for s in scores]
        )
        top = jnp.maximum(top, 0.1 * LOW)
        total = jnp.zeros_like(top)
        delta = jnp.zeros_like(top)
        for s, b in zip(scores, blocks):
            weight = jnp.exp2(s - top)
            dprobs = mm(b[:, cut2], dout, NT)
            total += jnp.sum(weight, axis=0, keepdims=True)
            delta += jnp.sum(weight * dprobs, axis=0, keepdims=True)
        total = jnp.maximum(total, 1.0)
        out_ref[h : h + 1, :] = top + jnp.log2(total)
        out_ref[8 + h : 9 + h, :] = delta / total


def grads_kernel(heads, valid_ref, *refs):
    rows_refs, frame_refs, stat_refs = refs[:4], refs[4:8], refs[8:12]
    keep_refs, send_ref = refs[12:14], refs[14]
    dq_refs = refs[15:19]
    width = heads * HD
    rows = jnp.concatenate([r[...] for r in rows_refs], axis=0)
    blocks = [r[...] for r in frame_refs]
    part = blocks[0].shape[0]
    own = rows_refs[0].shape[0]
    stats = [stat_refs[0][...]] + [
        pltpu.roll(stat_refs[k][...], own * k, 1) for k in (1, 2, 3)
    ]
    tops = [s[:8] for s in stats]
    top = functools.reduce(jnp.maximum, tops)
    shares = [jnp.exp2(t - top) for t in tops]
    total = functools.reduce(jnp.add, shares)
    lse = top + jnp.log2(total)
    delta = functools.reduce(
        jnp.add, [w * s[8:] for w, s in zip(shares, stats)]
    ) / total
    biases = [frame_bias(valid_ref, j, part) for j in range(4)]
    dq_t, att_t = [], []
    for h in range(heads):
        cut = slice(h * HD, (h + 1) * HD)
        cut2 = slice(width + h * HD, width + (h + 1) * HD)
        query, dout = rows[:, cut], rows[:, cut2]
        dq_sum = jnp.zeros((HD, rows.shape[0]), F32)
        att_sum = jnp.zeros((HD, rows.shape[0]), F32)
        for j, (b, bias) in enumerate(zip(blocks, biases)):
            key, value = b[:, cut], b[:, cut2]
            scores = mm(key, query, NT) * LOG2 + bias
            probs = jnp.exp2(scores - lse[h : h + 1])
            dprobs = mm(value, dout, NT)
            dscores = (probs * (dprobs - delta[h : h + 1])).astype(BF)
            probs = probs.astype(BF)
            dkey = mm(dscores, query) * SCALE
            dvalue = mm(probs, dout)
            out_ref = send_ref if j % 2 else keep_refs[j // 2]
            span = slice((j // 2) * part, (j // 2 + 1) * part) if j % 2 else slice(0, part)
            out_ref[span, cut] = dkey.astype(out_ref.dtype)
            out_ref[span, cut2] = dvalue.astype(out_ref.dtype)
            dq_sum += mm(key, dscores, TN)
            att_sum += mm(value, probs, TN)
        dq_t.append(dq_sum * SCALE)
        att_t.append(att_sum)
    joined = jnp.concatenate(dq_t + att_t, axis=0).T
    for k in range(4):
        dq_refs[k][...] = joined[k * own : (k + 1) * own].astype(dq_refs[k].dtype)


def project_kernel(left_ref, right_ref, w1_ref, w2_ref, out_ref):
    width = w1_ref.shape[0]
    out_ref[:, :width] = mm(left_ref[...], w1_ref[...], NT).astype(out_ref.dtype)
    out_ref[:, width:] = mm(right_ref[...], w2_ref[...], NT).astype(out_ref.dtype)


def frames_kernel(frames_ref, w1_ref, w2_ref, out_ref):
    project_kernel(frames_ref, frames_ref, w1_ref, w2_ref, out_ref)


def collect_kernel(keep_ref, core_ref, pair_ref, dq_ref, a_ref, b_ref, c_ref, out_ref):
    slab = keep_ref.shape[0]
    total = keep_ref[...] + core_ref[:slab].astype(F32) + pair_ref[...].astype(F32)
    out_ref[:slab] = total.astype(out_ref.dtype)
    total = dq_ref[...] + a_ref[...].astype(F32) + b_ref[...].astype(F32)
    out_ref[slab:] = (total + c_ref[...].astype(F32)).astype(out_ref.dtype)


def weights_kernel(part, xt_ref, xt2_ref, y_ref, y2_ref, *out_refs):
    kv_refs, keep_ref, send_ref = out_refs[:4], out_refs[4], out_refs[5]
    frames = y_ref.shape[0] - part
    half = y_ref.shape[1] // 2
    step = kv_refs[0].shape[0]
    pairs = ((xt_ref, y_ref), (xt2_ref, y2_ref))
    for k in (3, 1, 2, 0):
        span = slice(k * step, (k + 1) * step)
        kv = sum(mm(x[span, :frames], y[:frames, :]) for x, y in pairs)
        kv_refs[k][...] = kv.astype(kv_refs[k].dtype)
        q = sum(
            mm(x[span, frames : frames + part], y[frames:, :half]) for x, y in pairs
        )
        o = sum(mm(x[span, frames + part :], y[frames:, half:]) for x, y in pairs)
        near = slice(k * step // 2, (k + 1) * step // 2)
        keep_ref[near, :half] = q[: step // 2]
        keep_ref[near, half:] = o[: step // 2]
        send_ref[near, :half] = q[step // 2 :].astype(send_ref.dtype)
        send_ref[near, half:] = o[step // 2 :].astype(send_ref.dtype)


def inputs_kernel(where_ref, y_ref, wk_ref, wv_ref, wq_ref, own_ref, *refs):
    send_refs, scratch = refs[:3], refs[3]
    width = wk_ref.shape[0]
    frames = y_ref.shape[0] - (y_ref.shape[0] // 5)
    dkey, dvalue = y_ref[:frames, :width], y_ref[:frames, width:]
    dquery = y_ref[frames:, :width]
    for t in range(4):
        span = slice(t * width, (t + 1) * width)
        scratch[t, :frames] = mm(dkey, wk_ref[:, span]) + mm(dvalue, wv_ref[:, span])
        scratch[t, frames:] = mm(dquery, wq_ref[:, span])
    own_ref[...] = scratch[where_ref[0]]
    for k in (1, 2, 3):
        send_refs[k - 1][...] = scratch[lax.rem(where_ref[0] + k, 4)].astype(BF)


VMEM = pl.BlockSpec(memory_space=pltpu.VMEM)
SMEM = pl.BlockSpec(memory_space=pltpu.SMEM)
PARAMS = pltpu.CompilerParams(vmem_limit_bytes=24 * 1024 * 1024)


def per_device(query_in, grad_out, encoder_states, frame_lengths, w_query, w_key, w_value, w_out):
    rows_in, rows_grad, frames = query_in[0], grad_out[0], encoder_states[0]
    width = w_query.shape[1]
    heads = width // HD
    model = w_query.shape[0]
    own, slab = rows_in.shape[0], frames.shape[0]
    xi, ai, bi, ci, yi = (lax.axis_index(n) for n in ("dp", "a", "b", "core", "head"))

    wq_t, wk_t, wv_t = w_query.T, w_key.T, w_value.T
    rows0 = pl.pallas_call(
        project_kernel,
        out_shape=jax.ShapeDtypeStruct((own, 2 * width), BF),
        in_specs=[VMEM] * 4,
        out_specs=VMEM,
        compiler_params=PARAMS,
    )(rows_in, rows_grad, wq_t, w_out)
    row_blocks = [rows0] + [ring(rows0, "a", 4, j) for j in (2, 1, 3)]

    frames, rows0 = lax.optimization_barrier((frames, rows0))
    kv = pl.pallas_call(
        frames_kernel,
        out_shape=jax.ShapeDtypeStruct((slab, 2 * width), BF),
        in_specs=[VMEM] * 3,
        out_specs=VMEM,
        compiler_params=PARAMS,
    )(frames, wk_t, wv_t)
    kv_pair = swap(kv, "b")
    kv_core = swap(kv, "core")
    row_blocks[1:], kv_pair, kv_core = lax.optimization_barrier(
        (row_blocks[1:], kv_pair, kv_core)
    )
    row_blocks = [rows0, row_blocks[2], row_blocks[1], row_blocks[3]]
    frame_blocks = [kv, kv_core, kv_pair, swap(kv_pair, "core")]
    starts = [
        slab * (4 * ai + 2 * (bi ^ db) + (ci ^ dc)) for db in (0, 1) for dc in (0, 1)
    ]
    valid = jnp.stack([frame_lengths[0] - s for s in starts]).astype(jnp.int32)

    place = jnp.arange(model, dtype=jnp.int32)
    inner = model // 64
    rest, unit = place // inner, place % inner
    a_rel, b_rel = rest % 4, (rest // 4) % 2
    x_rel, c_rel = (rest // 8) % 4, rest // 32
    target = (
        ((x_rel + xi) % 4) * 16 + ((a_rel + ai) % 4) * 4 + (b_rel ^ bi) * 2 + (c_rel ^ ci)
    ) * inner + unit
    pick = (place[:, None] == target[None, :]).astype(BF)
    stacked = jnp.concatenate([frames, rows_in, rows_grad], axis=0)
    turned = mm(pick, stacked, (((0,), (1,)), ((), ()))).astype(BF)
    turned_own = turned[: model // 2]
    turned_other = swap(turned[model // 2 :], "core")

    stats = pl.pallas_call(
        functools.partial(stats_kernel, heads),
        out_shape=jax.ShapeDtypeStruct((16, 4 * own), F32),
        in_specs=[SMEM] + [VMEM] * 8,
        out_specs=VMEM,
        compiler_params=PARAMS,
    )(valid, *row_blocks, *frame_blocks)
    all_stats = [stats] + [ring(stats, "a", 4, j) for j in (1, 2, 3)]

    keep0, keep1, send, dq0, dq1, dq2, dq3 = pl.pallas_call(
        functools.partial(grads_kernel, heads),
        out_shape=[jax.ShapeDtypeStruct((slab, 2 * width), F32)] * 2
        + [
            jax.ShapeDtypeStruct((2 * slab, 2 * width), BF),
            jax.ShapeDtypeStruct((own, 2 * width), F32),
        ]
        + [jax.ShapeDtypeStruct((own, 2 * width), BF)] * 3,
        in_specs=[SMEM] + [VMEM] * 12,
        out_specs=[VMEM] * 7,
        compiler_params=PARAMS,
    )(valid, *row_blocks, *frame_blocks, *all_stats)

    recv = swap(send, "core")
    pair = (keep1 + recv[slab:].astype(F32)).astype(BF)
    dq2, dq1, dq3, pair = lax.optimization_barrier((dq2, dq1, dq3, pair))
    pair_recv = swap(pair, "b")
    dq_recv = [ring(d, "a", 4, -j) for j, d in ((2, dq2), (1, dq1), (3, dq3))]
    grads = pl.pallas_call(
        collect_kernel,
        out_shape=jax.ShapeDtypeStruct((slab + own, 2 * width), BF),
        in_specs=[VMEM] * 7,
        out_specs=VMEM,
        compiler_params=PARAMS,
    )(keep0, recv, pair_recv, dq0, *dq_recv)
    grads_other = swap(grads, "core")

    step = model // 8
    *kv_parts, qo_keep, qo_send = pl.pallas_call(
        functools.partial(weights_kernel, own),
        out_shape=[jax.ShapeDtypeStruct((step, 2 * width), F32)]
        + [jax.ShapeDtypeStruct((step, 2 * width), BF)] * 3
        + [
            jax.ShapeDtypeStruct((model // 4, 2 * width), F32),
            jax.ShapeDtypeStruct((model // 4, 2 * width), BF),
        ],
        in_specs=[VMEM] * 4,
        out_specs=[VMEM] * 6,
        compiler_params=PARAMS,
    )(turned_own, turned_other, grads, grads_other)
    kv_x = [ring(kv_parts[k], "dp", 4, k) for k in (2, 1, 3)]
    qo_b = swap(qo_send, "b")

    held, kv_parts[0] = lax.optimization_barrier((grads, kv_parts[0]))
    own_part, *parts = pl.pallas_call(
        inputs_kernel,
        out_shape=[jax.ShapeDtypeStruct((slab + own, width), F32)]
        + [jax.ShapeDtypeStruct((slab + own, width), BF)] * 3,
        in_specs=[SMEM] + [VMEM] * 4,
        out_specs=[VMEM] * 4,
        scratch_shapes=[pltpu.VMEM((4, slab + own, width), F32)],
        compiler_params=PARAMS,
    )(yi.reshape(1).astype(jnp.int32), held, wk_t, wv_t, wq_t)
    arrived = [ring(parts[k - 1], "head", 4, k) for k in (2, 1, 3)]

    cut = step // 2
    kv_sum = kv_parts[0] + sum(k.astype(F32) for k in kv_x)
    qo_sum = qo_keep + qo_b.astype(F32)
    kv_b = swap(kv_sum[cut:].astype(BF), "b")
    qo_x = [ring(qo_sum[k * cut : (k + 1) * cut].astype(BF), "dp", 4, k) for k in (2, 1, 3)]
    inputs = (own_part + sum(p.astype(F32) for p in arrived)).astype(BF)
    dframes, dinput = inputs[:slab], inputs[slab:]

    kv_sum = kv_sum[:cut] + kv_b.astype(F32)
    qo_sum = qo_sum[:cut] + sum(q.astype(F32) for q in qo_x)
    total = jnp.concatenate([kv_sum, qo_sum], axis=1)
    low = total.astype(BF)
    over_a = [ring(low[k * inner : (k + 1) * inner], "a", 4, k) for k in (2, 1, 3)]
    total = total[:inner] + sum(p.astype(F32) for p in over_a)
    return (
        dinput[None],
        dframes[None],
        total[:, 2 * width : 3 * width],
        total[:, :width],
        total[:, width : 2 * width],
        total[:, 3 * width :].T,
    )


def solution(mesh):
    dp, tm, head = mesh.devices.shape
    fine = Mesh(mesh.devices.reshape(dp, 4, 2, 2, head), ("dp", "a", "b", "core", "head"))
    tm = ("a", "b", "core")
    placed = (
        P("dp", tm, None),
        P("dp", tm, None),
        P("dp", tm, None),
        P("dp"),
        P(None, "head"),
        P(None, "head"),
        P(None, "head"),
        P("head", None),
    )
    every = ("dp",) + tm
    return jax.shard_map(
        per_device,
        mesh=fine,
        in_specs=placed,
        out_specs=(
            P("dp", tm, "head"),
            P("dp", tm, "head"),
            P(every, "head"),
            P(every, "head"),
            P(every, "head"),
            P("head", every),
        ),
        check_vma=False,
    )
```

```python
import functools
import math

import jax
import jax.numpy as jnp
from jax import lax
from jax.experimental import pallas as pl
from jax.experimental.pallas import tpu as pltpu
from jax.sharding import Mesh, PartitionSpec as P

HD = 64
BF = jnp.bfloat16
F32 = jnp.float32
SCALE = HD ** (-0.5)
LOG2 = SCALE * math.log2(math.e)
LOW = -1e30
NT = (((1,), (1,)), ((), ()))
TN = (((0,), (0,)), ((), ()))


def mm(left, right, dims=None):
    if dims is None:
        dims = (((1,), (0,)), ((), ()))
    return lax.dot_general(left, right, dims, preferred_element_type=F32)


def flip(x, axis, size, bits):
    return lax.ppermute(x, axis, [(i, i ^ bits) for i in range(size)])


def swap(x, axis):
    return flip(x, axis, 2, 1)


def frame_bias(valid_ref, block, rows):
    positions = lax.broadcasted_iota(jnp.int32, (rows, 1), 0)
    return jnp.where(positions < valid_ref[block], 0.0, LOW)


def stats_kernel(heads, valid_ref, *refs):
    rows_refs, frame_refs, out_ref = refs[:4], refs[4:8], refs[8]
    width = heads * HD
    rows = jnp.concatenate([r[...] for r in rows_refs], axis=0)
    blocks = [r[...] for r in frame_refs]
    biases = [frame_bias(valid_ref, j, b.shape[0]) for j, b in enumerate(blocks)]
    out_ref[...] = jnp.zeros_like(out_ref)
    for h in range(heads):
        cut = slice(h * HD, (h + 1) * HD)
        cut2 = slice(width + h * HD, width + (h + 1) * HD)
        query, dout = rows[:, cut], rows[:, cut2]
        scores = [
            mm(b[:, cut], query, NT) * LOG2 + bias for b, bias in zip(blocks, biases)
        ]
        top = functools.reduce(
            jnp.maximum, [jnp.max(s, axis=0, keepdims=True) for s in scores]
        )
        top = jnp.maximum(top, 0.1 * LOW)
        total = jnp.zeros_like(top)
        delta = jnp.zeros_like(top)
        for s, b in zip(scores, blocks):
            weight = jnp.exp2(s - top)
            dprobs = mm(b[:, cut2], dout, NT)
            total += jnp.sum(weight, axis=0, keepdims=True)
            delta += jnp.sum(weight * dprobs, axis=0, keepdims=True)
        total = jnp.maximum(total, 1.0)
        out_ref[h : h + 1, :] = top + jnp.log2(total)
        out_ref[8 + h : 9 + h, :] = delta / total


def in_own_order(x, k, own):
    if k & 2:
        x = pltpu.roll(x, 2 * own, 1)
    if k & 1:
        lane = lax.broadcasted_iota(jnp.int32, x.shape, 1)
        x = jnp.where(
            lane % (2 * own) < own, pltpu.roll(x, 3 * own, 1), pltpu.roll(x, own, 1)
        )
    return x


def grads_kernel(heads, valid_ref, *refs):
    rows_refs, frame_refs, stat_refs = refs[:4], refs[4:8], refs[8:12]
    dkv_ref, dq_refs = refs[12], refs[13:17]
    width = heads * HD
    rows = jnp.concatenate([r[...] for r in rows_refs], axis=0)
    blocks = [r[...] for r in frame_refs]
    part = blocks[0].shape[0]
    own = rows_refs[0].shape[0]
    stats = [in_own_order(stat_refs[k][...], k, own) for k in range(4)]
    tops = [s[:8] for s in stats]
    top = functools.reduce(jnp.maximum, tops)
    shares = [jnp.exp2(t - top) for t in tops]
    total = functools.reduce(jnp.add, shares)
    lse = top + jnp.log2(total)
    delta = functools.reduce(
        jnp.add, [w * s[8:] for w, s in zip(shares, stats)]
    ) / total
    biases = [frame_bias(valid_ref, j, part) for j in range(4)]
    dq_t, att_t = [], []
    for h in range(heads):
        cut = slice(h * HD, (h + 1) * HD)
        cut2 = slice(width + h * HD, width + (h + 1) * HD)
        query, dout = rows[:, cut], rows[:, cut2]
        dq_sum = jnp.zeros((HD, rows.shape[0]), F32)
        att_sum = jnp.zeros((HD, rows.shape[0]), F32)
        for j, (b, bias) in enumerate(zip(blocks, biases)):
            key, value = b[:, cut], b[:, cut2]
            scores = mm(key, query, NT) * LOG2 + bias
            probs = jnp.exp2(scores - lse[h : h + 1])
            dprobs = mm(value, dout, NT)
            dscores = (probs * (dprobs - delta[h : h + 1])).astype(BF)
            probs = probs.astype(BF)
            dkey = mm(dscores, query) * SCALE
            dvalue = mm(probs, dout)
            span = slice(j * part, (j + 1) * part)
            dkv_ref[span, cut] = dkey.astype(dkv_ref.dtype)
            dkv_ref[span, cut2] = dvalue.astype(dkv_ref.dtype)
            dq_sum += mm(key, dscores, TN)
            att_sum += mm(value, probs, TN)
        dq_t.append(dq_sum * SCALE)
        att_t.append(att_sum)
    joined = jnp.concatenate(dq_t + att_t, axis=0).T
    for k in range(4):
        dq_refs[k][...] = joined[k * own : (k + 1) * own].astype(dq_refs[k].dtype)


def fetch(pairs, sems):
    copies = [
        pltpu.make_async_copy(source, target, sems.at[i])
        for i, (source, target) in enumerate(pairs)
    ]
    for copy in copies:
        copy.start()
    return copies


def project_kernel(left_ref, right_ref, w1_ref, w2_ref, out_ref, left, right, w1, w2, sems):
    width = w1.shape[0]
    half = width // 2
    copies = fetch(
        [
            (left_ref, left),
            (w1_ref.at[:half], w1.at[:half]),
            (w1_ref.at[half:], w1.at[half:]),
            (right_ref, right),
            (w2_ref.at[:half], w2.at[:half]),
            (w2_ref.at[half:], w2.at[half:]),
        ],
        sems,
    )
    for copy in copies[:3]:
        copy.wait()
    out_ref[:, :width] = mm(left[...], w1[...], NT).astype(out_ref.dtype)
    for copy in copies[3:]:
        copy.wait()
    out_ref[:, width:] = mm(right[...], w2[...], NT).astype(out_ref.dtype)


def frames_kernel(frames_ref, w1_ref, w2_ref, out_ref):
    width = w1_ref.shape[0]
    out_ref[:, :width] = mm(frames_ref[...], w1_ref[...], NT).astype(out_ref.dtype)
    out_ref[:, width:] = mm(frames_ref[...], w2_ref[...], NT).astype(out_ref.dtype)


def pair_kernel(where_ref, e0_ref, e1_ref, e2_ref, e3_ref, w1_ref, w2_ref, out_ref, pair_ref):
    part = e0_ref.shape[0]
    for k, e_ref in enumerate((e0_ref, e1_ref, e2_ref, e3_ref)):
        start = pl.multiple_of((where_ref[0] ^ k) * part, part)
        pair_ref[pl.ds(start, part), :] = e_ref[...]
    frames_kernel(pair_ref, w1_ref, w2_ref, out_ref)


def chip_sum(own_ref, other_ref, block, rows):
    near = slice(block * rows, (block + 1) * rows)
    far = slice((block ^ 1) * rows, ((block ^ 1) + 1) * rows)
    return (own_ref[near].astype(F32) + other_ref[far].astype(F32)).astype(BF)


def kv_weights_kernel(xt_ref, xt2_ref, y_ref, y2_ref, *out_refs):
    part = y_ref.shape[0] // 4
    step = out_refs[0].shape[0]
    sums = [chip_sum(y_ref, y2_ref, j, part) for j in range(4)]
    near = jnp.concatenate([sums[0], sums[2]], axis=0)
    far = jnp.concatenate([sums[1], sums[3]], axis=0)
    for k in (2, 3, 1, 0):
        span = slice(k * step, (k + 1) * step)
        total = mm(xt_ref[span], near) + mm(xt2_ref[span], far)
        out_refs[k][...] = total.astype(out_refs[k].dtype)


def qo_weights_kernel(own, *refs):
    x_refs, y_ref, y2_ref, out_refs = refs[:4], refs[4], refs[5], refs[6:]
    half = y_ref.shape[1] // 2
    step = out_refs[0].shape[0]
    for k in (2, 3, 1, 0):
        span = slice(k * step, (k + 1) * step)
        for side in (0, 1):
            cols = slice(side * half, (side + 1) * half)
            total = jnp.zeros((step, half), F32)
            for j, x_ref in enumerate(x_refs):
                rows = slice(j * own, (j + 1) * own)
                for c, y in enumerate((y_ref, y2_ref)):
                    at = (2 * c + side) * own
                    total += mm(x_ref[span, at : at + own], y[rows, cols])
            out_refs[k][:, cols] = total.astype(out_refs[k].dtype)


def inputs_kernel(where_ref, y_ref, y2_ref, dq_ref, wk_ref, wv_ref, wq_ref, own_ref, *refs):
    send_refs, scratch = refs[:3], refs[3]
    width = wk_ref.shape[0]
    part = y_ref.shape[0] // 4
    dkv = jnp.concatenate(
        [chip_sum(y_ref, y2_ref, 0, part), chip_sum(y_ref, y2_ref, 2, part)], axis=0
    )
    dkey, dvalue, dquery = dkv[:, :width], dkv[:, width:], dq_ref[:, :width]
    for t in range(4):
        span = slice(t * width, (t + 1) * width)
        scratch[t, : 2 * part] = mm(dkey, wk_ref[:, span]) + mm(dvalue, wv_ref[:, span])
        scratch[t, 2 * part :] = mm(dquery, wq_ref[:, span])
    own_ref[...] = scratch[where_ref[0]]
    for k in (1, 2, 3):
        send_refs[k - 1][...] = scratch[where_ref[0] ^ k].astype(BF)


VMEM = pl.BlockSpec(memory_space=pltpu.VMEM)
SMEM = pl.BlockSpec(memory_space=pltpu.SMEM)


def per_device(query_in, grad_out, encoder_states, frame_lengths, w_query, w_key, w_value, w_out):
    rows_in, rows_grad, frames = query_in[0], grad_out[0], encoder_states[0]
    width = w_query.shape[1]
    heads = width // HD
    model = w_query.shape[0]
    inner = model // 64
    own, slab = rows_in.shape[0], frames.shape[0]
    quarter = slab // 4
    xi, zi, ci, yi = (lax.axis_index(n) for n in ("dp", "z", "core", "head"))
    wq_t, wk_t, wv_t = w_query.T, w_key.T, w_value.T
    where = yi.reshape(1).astype(jnp.int32)

    def call(kernel, outs, ins, scalar=False, scratch=(), limit=24):
        shapes = [jax.ShapeDtypeStruct(shape, kind) for shape, kind in outs]
        specs = [SMEM] * scalar + [VMEM] * (len(ins) - scalar)
        return pl.pallas_call(
            kernel,
            out_shape=shapes,
            in_specs=specs,
            out_specs=[VMEM] * len(outs),
            scratch_shapes=scratch,
            compiler_params=pltpu.CompilerParams(vmem_limit_bytes=limit * 1024 * 1024),
        )(*ins)

    e_part = flip(lax.dynamic_slice_in_dim(frames, yi * quarter, quarter, 0), "z", 8, 7)
    e_parts = [e_part] + [flip(e_part, "head", 4, k) for k in (1, 2, 3)]

    (rows0,) = pl.pallas_call(
        project_kernel,
        out_shape=[jax.ShapeDtypeStruct((own, 2 * width), BF)],
        in_specs=[pl.BlockSpec(memory_space=pl.ANY)] * 4,
        out_specs=[VMEM],
        scratch_shapes=[
            pltpu.VMEM((own, model), BF),
            pltpu.VMEM((own, model), BF),
            pltpu.VMEM((width, model), BF),
            pltpu.VMEM((width, model), BF),
            pltpu.SemaphoreType.DMA((6,)),
        ],
        compiler_params=pltpu.CompilerParams(vmem_limit_bytes=56 * 1024 * 1024),
    )(rows_in, rows_grad, wq_t, w_out)
    row_blocks = [rows0] + [flip(rows0, "z", 8, j) for j in (1, 2, 3)]

    (kv,) = call(frames_kernel, [((slab, 2 * width), BF)], (frames, wk_t, wv_t))
    kv_core = swap(kv, "core")
    kv_pair, e_pair = call(
        pair_kernel,
        [((slab, 2 * width), BF), ((slab, model), BF)],
        (where, *e_parts, wk_t, wv_t),
        True,
    )
    frame_blocks = [kv, kv_core, kv_pair, swap(kv_pair, "core")]
    starts = [
        slab * (2 * (zi ^ (7 * db)) + (ci ^ dc)) for db in (0, 1) for dc in (0, 1)
    ]
    valid = jnp.stack([frame_lengths[0] - s for s in starts]).astype(jnp.int32)

    (stats,) = call(
        functools.partial(stats_kernel, heads),
        [((16, 4 * own), F32)],
        (valid, *row_blocks, *frame_blocks),
        True,
    )
    all_stats = [stats] + [flip(stats, "z", 8, j) for j in (1, 2, 3)]

    def turn(order, stacked):
        place = jnp.arange(model, dtype=jnp.int32)
        unit, rest, rel = place % inner, place // inner, {}
        for name, size in reversed(order):
            rel[name], rest = rest % size, rest // size
        target = (
            (rel["x"] ^ xi) * 16 + (rel["a"] ^ (7 * rel["b"]) ^ zi) * 2 + (rel["c"] ^ ci)
        ) * inner + unit
        pick = (place[:, None] == target[None, :]).astype(BF)
        return mm(pick, stacked, (((0,), (1,)), ((), ()))).astype(BF)

    turned = turn(
        (("c", 2), ("x", 4), ("a", 4), ("b", 2)),
        jnp.concatenate([frames, e_pair], axis=0),
    )
    xt = turned[: model // 2]
    xt_other = swap(turned[model // 2 :], "core")
    turned = turn(
        (("c", 2), ("a", 4), ("x", 4), ("b", 2)),
        jnp.concatenate([rows_in, rows_grad], axis=0),
    )
    xq = jnp.concatenate(
        [turned[: model // 2], swap(turned[model // 2 :], "core")], axis=1
    )
    all_stats[1:], xt, xt_other, xq = lax.optimization_barrier(
        (all_stats[1:], xt, xt_other, xq)
    )
    part = model // 8
    xq_blocks = [xq[:part]] + [
        flip(xq[k * part : (k + 1) * part], "z", 8, k) for k in (1, 2, 3)
    ]

    dkv, dq0, *dq_sends = call(
        functools.partial(grads_kernel, heads),
        [((4 * slab, 2 * width), BF), ((own, 2 * width), F32)]
        + [((own, 2 * width), BF)] * 3,
        (valid, *row_blocks, *frame_blocks, *all_stats),
        True,
    )

    dkv_other = swap(dkv, "core")
    dq_recv = [flip(d, "z", 8, k) for k, d in zip((1, 2, 3), dq_sends)]
    kv_own, *kv_sends = call(
        kv_weights_kernel,
        [((part, 2 * width), F32)] + [((part, 2 * width), BF)] * 3,
        (xt, xt_other, dkv, dkv_other),
    )
    kv_x = [flip(kv_sends[k - 1], "dp", 4, k) for k in (1, 2, 3)]

    dqo = (dq0 + sum(d.astype(F32) for d in dq_recv)).astype(BF)
    dqo, kv_own = lax.optimization_barrier((dqo, kv_own))
    quad = jnp.concatenate([dqo] + [flip(dqo, "z", 8, k) for k in (1, 2, 3)], axis=0)
    quad_other = swap(quad, "core")

    own_part, *sends = call(
        inputs_kernel,
        [((2 * slab + own, width), F32)] + [((2 * slab + own, width), BF)] * 3,
        (where, dkv, dkv_other, dqo, wk_t, wv_t, wq_t),
        True,
        [pltpu.VMEM((4, 2 * slab + own, width), F32)],
    )
    arrived = [flip(sends[k - 1], "head", 4, k) for k in (1, 2, 3)]

    kv_sum = kv_own + sum(k.astype(F32) for k in kv_x)
    low = kv_sum.astype(BF)
    cut = 2 * inner
    kv_a = [flip(low[k * cut : (k + 1) * cut], "z", 8, k) for k in (1, 2, 3)]

    qo_parts = call(
        functools.partial(qo_weights_kernel, own),
        [((cut, 2 * width), F32)] + [((cut, 2 * width), BF)] * 3,
        (*xq_blocks, quad, quad_other),
    )
    qo_x = [flip(qo_parts[k], "dp", 4, k) for k in (1, 2, 3)]

    inputs = own_part + sum(p.astype(F32) for p in arrived)
    pair = flip(inputs[slab : 2 * slab].astype(BF), "z", 8, 7)
    dframes = (inputs[:slab] + pair.astype(F32)).astype(BF)
    dinput = inputs[2 * slab :].astype(BF)

    kv_sum = kv_sum[:cut] + sum(k.astype(F32) for k in kv_a)
    qo_sum = qo_parts[0] + sum(q.astype(F32) for q in qo_x)
    total = jnp.concatenate([kv_sum, qo_sum], axis=1)
    total = total[:inner] + flip(total[inner:].astype(BF), "z", 8, 7).astype(F32)
    return (
        dinput[None],
        dframes[None],
        total[:, 2 * width : 3 * width],
        total[:, :width],
        total[:, width : 2 * width],
        total[:, 3 * width :].T,
    )


def solution(mesh):
    dp, tm, head = mesh.devices.shape
    fine = Mesh(mesh.devices.reshape(dp, tm // 2, 2, head), ("dp", "z", "core", "head"))
    tm = ("z", "core")
    placed = (
        P("dp", tm, None),
        P("dp", tm, None),
        P("dp", tm, None),
        P("dp"),
        P(None, "head"),
        P(None, "head"),
        P(None, "head"),
        P("head", None),
    )
    every = ("dp",) + tm
    return jax.shard_map(
        per_device,
        mesh=fine,
        in_specs=placed,
        out_specs=(
            P("dp", tm, "head"),
            P("dp", tm, "head"),
            P(every, "head"),
            P(every, "head"),
            P(every, "head"),
            P("head", every),
        ),
        check_vma=False,
    )
```

```python
import functools
import math

import jax
import jax.numpy as jnp
from jax import lax
from jax.experimental import pallas as pl
from jax.experimental.pallas import tpu as pltpu
from jax.sharding import Mesh, PartitionSpec as P

HD = 64
BF = jnp.bfloat16
F32 = jnp.float32
SCALE = HD ** (-0.5)
LOG2 = SCALE * math.log2(math.e)
LOW = -1e30
NT = (((1,), (1,)), ((), ()))
TN = (((0,), (0,)), ((), ()))


def mm(left, right, dims=None):
    if dims is None:
        dims = (((1,), (0,)), ((), ()))
    return lax.dot_general(left, right, dims, preferred_element_type=F32)


def flip(x, axis, size, bits):
    return lax.ppermute(x, axis, [(i, i ^ bits) for i in range(size)])


def swap(x, axis):
    return flip(x, axis, 2, 1)


def frame_bias(valid_ref, block, rows):
    positions = lax.broadcasted_iota(jnp.int32, (rows, 1), 0)
    return jnp.where(positions < valid_ref[block], 0.0, LOW)


def stats_kernel(heads, valid_ref, *refs):
    rows_refs, frame_refs, out_ref = refs[:4], refs[4:8], refs[8]
    width = heads * HD
    rows = jnp.concatenate([r[...] for r in rows_refs], axis=0)
    blocks = [r[...] for r in frame_refs]
    biases = [frame_bias(valid_ref, j, b.shape[0]) for j, b in enumerate(blocks)]
    out_ref[...] = jnp.zeros_like(out_ref)
    for h in range(heads):
        cut = slice(h * HD, (h + 1) * HD)
        cut2 = slice(width + h * HD, width + (h + 1) * HD)
        query, dout = rows[:, cut], rows[:, cut2]
        scores = [
            mm(b[:, cut], query, NT) * LOG2 + bias for b, bias in zip(blocks, biases)
        ]
        top = functools.reduce(
            jnp.maximum, [jnp.max(s, axis=0, keepdims=True) for s in scores]
        )
        top = jnp.maximum(top, 0.1 * LOW)
        total = jnp.zeros_like(top)
        delta = jnp.zeros_like(top)
        for s, b in zip(scores, blocks):
            weight = jnp.exp2(s - top)
            dprobs = mm(b[:, cut2], dout, NT)
            total += jnp.sum(weight, axis=0, keepdims=True)
            delta += jnp.sum(weight * dprobs, axis=0, keepdims=True)
        total = jnp.maximum(total, 1.0)
        out_ref[h : h + 1, :] = top + jnp.log2(total)
        out_ref[8 + h : 9 + h, :] = delta / total


def in_own_order(x, k, own):
    if k & 2:
        x = pltpu.roll(x, 2 * own, 1)
    if k & 1:
        lane = lax.broadcasted_iota(jnp.int32, x.shape, 1)
        x = jnp.where(
            lane % (2 * own) < own, pltpu.roll(x, 3 * own, 1), pltpu.roll(x, own, 1)
        )
    return x


def grads_kernel(heads, valid_ref, *refs):
    rows_refs, frame_refs, stat_refs = refs[:4], refs[4:8], refs[8:12]
    dkv_ref, dq_refs = refs[12], refs[13:17]
    width = heads * HD
    rows = jnp.concatenate([r[...] for r in rows_refs], axis=0)
    blocks = [r[...] for r in frame_refs]
    part = blocks[0].shape[0]
    own = rows_refs[0].shape[0]
    stats = [in_own_order(stat_refs[k][...], k, own) for k in range(4)]
    tops = [s[:8] for s in stats]
    top = functools.reduce(jnp.maximum, tops)
    shares = [jnp.exp2(t - top) for t in tops]
    total = functools.reduce(jnp.add, shares)
    lse = top + jnp.log2(total)
    delta = functools.reduce(
        jnp.add, [w * s[8:] for w, s in zip(shares, stats)]
    ) / total
    biases = [frame_bias(valid_ref, j, part) for j in range(4)]
    dq_t, att_t = [], []
    for h in range(heads):
        cut = slice(h * HD, (h + 1) * HD)
        cut2 = slice(width + h * HD, width + (h + 1) * HD)
        query, dout = rows[:, cut], rows[:, cut2]
        dq_sum = jnp.zeros((HD, rows.shape[0]), F32)
        att_sum = jnp.zeros((HD, rows.shape[0]), F32)
        for j, (b, bias) in enumerate(zip(blocks, biases)):
            key, value = b[:, cut], b[:, cut2]
            scores = mm(key, query, NT) * LOG2 + bias
            probs = jnp.exp2(scores - lse[h : h + 1])
            dprobs = mm(value, dout, NT)
            dscores = (probs * (dprobs - delta[h : h + 1])).astype(BF)
            probs = probs.astype(BF)
            dkey = mm(dscores, query) * SCALE
            dvalue = mm(probs, dout)
            span = slice(j * part, (j + 1) * part)
            dkv_ref[span, cut] = dkey.astype(dkv_ref.dtype)
            dkv_ref[span, cut2] = dvalue.astype(dkv_ref.dtype)
            dq_sum += mm(key, dscores, TN)
            att_sum += mm(value, probs, TN)
        dq_t.append(dq_sum * SCALE)
        att_t.append(att_sum)
    joined = jnp.concatenate(dq_t + att_t, axis=0).T
    for k in range(4):
        dq_refs[k][...] = joined[k * own : (k + 1) * own].astype(dq_refs[k].dtype)


def fetch(pairs, sems):
    copies = [
        pltpu.make_async_copy(source, target, sems.at[i])
        for i, (source, target) in enumerate(pairs)
    ]
    for copy in copies:
        copy.start()
    return copies


def project_kernel(
    left_ref, right_ref, frames_ref, wq_ref, wo_ref, wk_ref, wv_ref, rows_ref, kv_ref,
    left, right, frames, wq, wo, wk, wv, sems,
):
    width = wq.shape[0]
    half = width // 2
    pairs = [(left_ref, left)]
    for source, target in ((wq_ref, wq), (wo_ref, wo), (wk_ref, wk), (wv_ref, wv)):
        pairs += [
            (source.at[:half], target.at[:half]),
            (source.at[half:], target.at[half:]),
        ]
        if source is wq_ref:
            pairs.append((right_ref, right))
        if source is wo_ref:
            pairs.append((frames_ref, frames))
    copies = fetch(pairs, sems)
    for i, (x, w, out, side) in enumerate(
        ((left, wq, rows_ref, 0), (right, wo, rows_ref, 1), (frames, wk, kv_ref, 0), (frames, wv, kv_ref, 1))
    ):
        for copy in copies[3 * i : 3 * i + 3]:
            copy.wait()
        out[:, side * width : (side + 1) * width] = mm(x[...], w[...], NT).astype(BF)


def kv_weights_kernel(xt_ref, xt2_ref, xp_ref, xp2_ref, y_ref, y2_ref, *out_refs):
    part = y_ref.shape[0] // 4
    step = out_refs[0].shape[0]
    sums = []
    for j in range(4):
        near = slice(j * part, (j + 1) * part)
        far = slice((j ^ 1) * part, ((j ^ 1) + 1) * part)
        total = y_ref[near].astype(F32) + y2_ref[far].astype(F32)
        if j == 0:
            out_refs[4][...] = total
        sums.append(total.astype(BF))
    out_refs[5][...] = sums[2]
    for k in (2, 3, 1, 0):
        span = slice(k * step, (k + 1) * step)
        total = mm(xt_ref[span, :part], sums[0]) + mm(xt2_ref[span, :part], sums[1])
        total += mm(xp_ref[span], sums[2]) + mm(xp2_ref[span], sums[3])
        out_refs[k][...] = total.astype(out_refs[k].dtype)


def qo_weights_kernel(xt_ref, xt2_ref, y_ref, y2_ref, *out_refs):
    own = y_ref.shape[0]
    half = y_ref.shape[1] // 2
    step = out_refs[0].shape[0]
    first = xt_ref.shape[1] - 2 * own
    for k in (2, 3, 1, 0):
        span = slice(k * step, (k + 1) * step)
        for side in (0, 1):
            cols = slice(side * half, (side + 1) * half)
            at = slice(first + side * own, first + (side + 1) * own)
            total = mm(xt_ref[span, at], y_ref[:, cols]) + mm(xt2_ref[span, at], y2_ref[:, cols])
            out_refs[k][:, cols] = total.astype(out_refs[k].dtype)


def inputs_kernel(where_ref, near_ref, pair_ref, dq_ref, wk_ref, wv_ref, wq_ref, own_ref, *refs):
    send_refs, scratch = refs[:3], refs[3]
    width = wk_ref.shape[0]
    part = near_ref.shape[0]
    dkv = (near_ref[...] + pair_ref[...].astype(F32)).astype(BF)
    dkey, dvalue, dquery = dkv[:, :width], dkv[:, width:], dq_ref[:, :width]
    for t in range(4):
        span = slice(t * width, (t + 1) * width)
        scratch[t, :part] = mm(dkey, wk_ref[:, span]) + mm(dvalue, wv_ref[:, span])
        scratch[t, part:] = mm(dquery, wq_ref[:, span])
    own_ref[...] = scratch[where_ref[0]]
    for k in (1, 2, 3):
        send_refs[k - 1][...] = scratch[where_ref[0] ^ k].astype(BF)


VMEM = pl.BlockSpec(memory_space=pltpu.VMEM)
SMEM = pl.BlockSpec(memory_space=pltpu.SMEM)


def per_device(query_in, grad_out, encoder_states, frame_lengths, w_query, w_key, w_value, w_out):
    rows_in, rows_grad, frames = query_in[0], grad_out[0], encoder_states[0]
    width = w_query.shape[1]
    heads = width // HD
    model = w_query.shape[0]
    inner = model // 64
    own, slab = rows_in.shape[0], frames.shape[0]
    quarter = slab // 4
    xi, zi, ci, yi = (lax.axis_index(n) for n in ("dp", "z", "core", "head"))
    wq_t, wk_t, wv_t = w_query.T, w_key.T, w_value.T
    where = yi.reshape(1).astype(jnp.int32)

    def call(kernel, outs, ins, scalar=False, scratch=(), work=2):
        shapes = [jax.ShapeDtypeStruct(shape, kind) for shape, kind in outs]
        specs = [SMEM] * scalar + [VMEM] * (len(ins) - scalar)
        return pl.pallas_call(
            kernel,
            out_shape=shapes,
            in_specs=specs,
            out_specs=[VMEM] * len(outs),
            scratch_shapes=scratch,
            compiler_params=pltpu.CompilerParams(vmem_limit_bytes=24 * 1024 * 1024),
            cost_estimate=pl.CostEstimate(
                flops=int(work * 1e9), bytes_accessed=0, transcendentals=0
            ),
        )(*ins)

    hbm = pl.BlockSpec(memory_space=pl.ANY)
    weights = [pltpu.VMEM((width, model), BF)] * 4
    rows0, kv = pl.pallas_call(
        project_kernel,
        out_shape=[
            jax.ShapeDtypeStruct((own, 2 * width), BF),
            jax.ShapeDtypeStruct((slab, 2 * width), BF),
        ],
        in_specs=[hbm] * 7,
        out_specs=[VMEM] * 2,
        scratch_shapes=[pltpu.VMEM((rows, model), BF) for rows in (own, own, slab)]
        + weights
        + [pltpu.SemaphoreType.DMA((12,))],
        compiler_params=pltpu.CompilerParams(vmem_limit_bytes=56 * 1024 * 1024),
    )(rows_in, rows_grad, frames, wq_t, w_out, wk_t, wv_t)

    kv_pair = flip(kv, "z", 8, 1)
    kv_core = swap(kv, "core")
    row_blocks = [rows0] + [flip(rows0, "z", 8, 2 * j) for j in (1, 2, 3)]

    def turn(stacked, other):
        place = jnp.arange(model, dtype=jnp.int32)
        unit, rest = place % inner, place // inner
        a_rel, b_rel = rest % 4, ((rest // 4) % 2) ^ other
        x_rel, c_rel = (rest // 8) % 4, rest // 32
        target = (
            (x_rel ^ xi) * 16 + ((2 * a_rel + b_rel) ^ zi) * 2 + (c_rel ^ ci)
        ) * inner + unit
        pick = (place[:, None] == target[None, :]).astype(BF)
        return mm(pick, stacked, (((0,), (1,)), ((), ()))).astype(BF)

    turned = turn(jnp.concatenate([frames, rows_in, rows_grad], axis=0), 0)
    for_pair = turn(frames, 1)
    row_blocks[1:], kv_pair, kv_core, for_pair, turned = lax.optimization_barrier(
        (row_blocks[1:], kv_pair, kv_core, for_pair, turned)
    )
    xt, xt_other = turned[: model // 2], swap(turned[model // 2 :], "core")
    frame_blocks = [kv, kv_core, kv_pair, swap(kv_pair, "core")]
    from_pair = flip(for_pair, "z", 8, 1)
    starts = [
        slab * (2 * (zi ^ db) + (ci ^ dc)) for db in (0, 1) for dc in (0, 1)
    ]
    valid = jnp.stack([frame_lengths[0] - s for s in starts]).astype(jnp.int32)

    (stats,) = call(
        functools.partial(stats_kernel, heads),
        [((16, 4 * own), F32)],
        (valid, *row_blocks, *frame_blocks),
        True,
        work=3,
    )
    all_stats = [stats] + [flip(stats, "z", 8, 2 * j) for j in (1, 2, 3)]

    all_stats[1:], from_pair, xt_other = lax.optimization_barrier(
        (all_stats[1:], from_pair, xt_other)
    )
    xp, xp_other = from_pair[: model // 2], swap(from_pair[model // 2 :], "core")

    dkv, dq0, *dq_sends = call(
        functools.partial(grads_kernel, heads),
        [((4 * slab, 2 * width), BF), ((own, 2 * width), F32)]
        + [((own, 2 * width), BF)] * 3,
        (valid, *row_blocks, *frame_blocks, *all_stats),
        True,
        work=8,
    )

    dkv_other = swap(dkv, "core")
    dq_recv = [flip(d, "z", 8, 2 * k) for k, d in zip((1, 2, 3), dq_sends)]

    part = model // 8
    kv_own, *kv_sends, near, pair = call(
        kv_weights_kernel,
        [((part, 2 * width), F32)]
        + [((part, 2 * width), BF)] * 3
        + [((slab, 2 * width), F32), ((slab, 2 * width), BF)],
        (xt, xt_other, xp, xp_other, dkv, dkv_other),
    )
    kv_x = [flip(kv_sends[k - 1], "dp", 4, k) for k in (2, 1, 3)]
    pair_recv = flip(pair, "z", 8, 1)

    dq_recv, kv_own = lax.optimization_barrier((dq_recv, kv_own))
    dqo = (dq0 + sum(d.astype(F32) for d in dq_recv)).astype(BF)
    dqo_other = swap(dqo, "core")
    qo_own, *qo_sends = call(
        qo_weights_kernel,
        [((part, 2 * width), F32)] + [((part, 2 * width), BF)] * 3,
        (xt, xt_other, dqo, dqo_other),
    )
    qo_x = [flip(qo_sends[k - 1], "dp", 4, k) for k in (2, 1, 3)]

    own_part, *sends = call(
        inputs_kernel,
        [((slab + own, width), F32)] + [((slab + own, width), BF)] * 3,
        (where, near, pair_recv, dqo, wk_t, wv_t, wq_t),
        True,
        [pltpu.VMEM((4, slab + own, width), F32)],
    )
    arrived = [flip(sends[k - 1], "head", 4, k) for k in (2, 1, 3)]
    inputs = (own_part + sum(p.astype(F32) for p in arrived)).astype(BF)
    dframes, dinput = inputs[:slab], inputs[slab:]

    kv_sum = kv_own + sum(k.astype(F32) for k in kv_x)
    qo_sum = qo_own + sum(k.astype(F32) for k in qo_x)
    total = jnp.concatenate([kv_sum, qo_sum], axis=1)
    cut = part // 2
    total = total[:cut] + flip(total[cut:].astype(BF), "z", 8, 1).astype(F32)
    low = total.astype(BF)
    over = [flip(low[k * inner : (k + 1) * inner], "z", 8, 2 * k) for k in (2, 1, 3)]
    total = total[:inner] + sum(p.astype(F32) for p in over)
    return (
        dinput[None],
        dframes[None],
        total[:, 2 * width : 3 * width],
        total[:, :width],
        total[:, width : 2 * width],
        total[:, 3 * width :].T,
    )


def solution(mesh):
    dp, tm, head = mesh.devices.shape
    fine = Mesh(mesh.devices.reshape(dp, tm // 2, 2, head), ("dp", "z", "core", "head"))
    tm = ("z", "core")
    placed = (
        P("dp", tm, None),
        P("dp", tm, None),
        P("dp", tm, None),
        P("dp"),
        P(None, "head"),
        P(None, "head"),
        P(None, "head"),
        P("head", None),
    )
    every = ("dp",) + tm
    return jax.shard_map(
        per_device,
        mesh=fine,
        in_specs=placed,
        out_specs=(
            P("dp", tm, "head"),
            P("dp", tm, "head"),
            P(every, "head"),
            P(every, "head"),
            P(every, "head"),
            P("head", every),
        ),
        check_vma=False,
    )
```

```python
import functools
import math

import jax
import jax.numpy as jnp
from jax import lax
from jax.experimental import pallas as pl
from jax.experimental.pallas import tpu as pltpu
from jax.sharding import Mesh, PartitionSpec as P

HD = 64
BF = jnp.bfloat16
F32 = jnp.float32
SCALE = HD ** (-0.5)
LOG2 = SCALE * math.log2(math.e)
LOW = -1e30
NT = (((1,), (1,)), ((), ()))
TN = (((0,), (0,)), ((), ()))


def mm(left, right, dims=None):
    if dims is None:
        dims = (((1,), (0,)), ((), ()))
    return lax.dot_general(left, right, dims, preferred_element_type=F32)


def flip(x, axis, size, bits):
    return lax.ppermute(x, axis, [(i, i ^ bits) for i in range(size)])


def swap(x, axis):
    return flip(x, axis, 2, 1)


def frame_bias(valid_ref, block, rows):
    positions = lax.broadcasted_iota(jnp.int32, (rows, 1), 0)
    return jnp.where(positions < valid_ref[block], 0.0, LOW)


def frame_blocks(refs):
    part = refs[0].shape[0] // 2
    return [r[db * part : (db + 1) * part, :] for db in (0, 1) for r in refs]


def stats_kernel(heads, valid_ref, *refs):
    rows_refs, frame_refs, out_ref = refs[:4], refs[4:6], refs[6]
    width = heads * HD
    rows = jnp.concatenate([r[...] for r in rows_refs], axis=0)
    blocks = frame_blocks(frame_refs)
    biases = [frame_bias(valid_ref, j, b.shape[0]) for j, b in enumerate(blocks)]
    out_ref[...] = jnp.zeros_like(out_ref)
    for h in range(heads):
        cut = slice(h * HD, (h + 1) * HD)
        cut2 = slice(width + h * HD, width + (h + 1) * HD)
        query, dout = rows[:, cut], rows[:, cut2]
        scores = [
            mm(b[:, cut], query, NT) * LOG2 + bias for b, bias in zip(blocks, biases)
        ]
        top = functools.reduce(
            jnp.maximum, [jnp.max(s, axis=0, keepdims=True) for s in scores]
        )
        top = jnp.maximum(top, 0.1 * LOW)
        total = jnp.zeros_like(top)
        delta = jnp.zeros_like(top)
        for s, b in zip(scores, blocks):
            weight = jnp.exp2(s - top)
            dprobs = mm(b[:, cut2], dout, NT)
            total += jnp.sum(weight, axis=0, keepdims=True)
            delta += jnp.sum(weight * dprobs, axis=0, keepdims=True)
        total = jnp.maximum(total, 1.0)
        out_ref[h : h + 1, :] = top + jnp.log2(total)
        out_ref[8 + h : 9 + h, :] = delta / total


def in_own_order(x, k, own):
    if k & 2:
        x = pltpu.roll(x, 2 * own, 1)
    if k & 1:
        lane = lax.broadcasted_iota(jnp.int32, x.shape, 1)
        x = jnp.where(
            lane % (2 * own) < own, pltpu.roll(x, 3 * own, 1), pltpu.roll(x, own, 1)
        )
    return x


def grads_kernel(heads, valid_ref, *refs):
    rows_refs, frame_refs, stat_refs = refs[:4], refs[4:6], refs[6:10]
    dkv_ref, dq_refs = refs[10], refs[11:15]
    width = heads * HD
    rows = jnp.concatenate([r[...] for r in rows_refs], axis=0)
    blocks = frame_blocks(frame_refs)
    part = blocks[0].shape[0]
    own = rows_refs[0].shape[0]
    stats = [in_own_order(stat_refs[k][...], k, own) for k in range(4)]
    tops = [s[:8] for s in stats]
    top = functools.reduce(jnp.maximum, tops)
    shares = [jnp.exp2(t - top) for t in tops]
    total = functools.reduce(jnp.add, shares)
    lse = top + jnp.log2(total)
    delta = functools.reduce(
        jnp.add, [w * s[8:] for w, s in zip(shares, stats)]
    ) / total
    biases = [frame_bias(valid_ref, j, part) for j in range(4)]
    dq_t, att_t = [], []
    for h in range(heads):
        cut = slice(h * HD, (h + 1) * HD)
        cut2 = slice(width + h * HD, width + (h + 1) * HD)
        query, dout = rows[:, cut], rows[:, cut2]
        dq_sum = jnp.zeros((HD, rows.shape[0]), F32)
        att_sum = jnp.zeros((HD, rows.shape[0]), F32)
        for j, (b, bias) in enumerate(zip(blocks, biases)):
            key, value = b[:, cut], b[:, cut2]
            scores = mm(key, query, NT) * LOG2 + bias
            probs = jnp.exp2(scores - lse[h : h + 1])
            dprobs = mm(value, dout, NT)
            dscores = (probs * (dprobs - delta[h : h + 1])).astype(BF)
            probs = probs.astype(BF)
            dkey = mm(dscores, query) * SCALE
            dvalue = mm(probs, dout)
            span = slice(j * part, (j + 1) * part)
            dkv_ref[span, cut] = dkey.astype(dkv_ref.dtype)
            dkv_ref[span, cut2] = dvalue.astype(dkv_ref.dtype)
            dq_sum += mm(key, dscores, TN)
            att_sum += mm(value, probs, TN)
        dq_t.append(dq_sum * SCALE)
        att_t.append(att_sum)
    joined = jnp.concatenate(dq_t + att_t, axis=0).T
    for k in range(4):
        dq_refs[k][...] = joined[k * own : (k + 1) * own].astype(dq_refs[k].dtype)


def fetch(pairs, sems):
    copies = [
        pltpu.make_async_copy(source, target, sems.at[i])
        for i, (source, target) in enumerate(pairs)
    ]
    for copy in copies:
        copy.start()
    return copies


def project_kernel(
    where_ref, left_ref, right_ref, frames_ref, wq_ref, wo_ref, wk_ref, wv_ref,
    rows_ref, kv_ref, quarter_ref, left, right, frames, wq, wo, wk, wv, sems,
):
    width = wq.shape[0]
    half = width // 2
    pairs = [(left_ref, left)]
    for source, target in ((wq_ref, wq), (wo_ref, wo), (wk_ref, wk), (wv_ref, wv)):
        pairs += [
            (source.at[:half], target.at[:half]),
            (source.at[half:], target.at[half:]),
        ]
        if source is wq_ref:
            pairs.append((right_ref, right))
        if source is wo_ref:
            pairs.append((frames_ref, frames))
    copies = fetch(pairs, sems)
    part = quarter_ref.shape[0]
    for i, (x, w, out, side) in enumerate(
        ((left, wq, rows_ref, 0), (right, wo, rows_ref, 1), (frames, wk, kv_ref, 0), (frames, wv, kv_ref, 1))
    ):
        for copy in copies[3 * i : 3 * i + 3]:
            copy.wait()
        if i == 2:
            start = pl.multiple_of(where_ref[0] * part, part)
            quarter_ref[...] = frames[pl.ds(start, part), :]
        out[:, side * width : (side + 1) * width] = mm(x[...], w[...], NT).astype(BF)


def pair_kernel(
    where_ref, e0_ref, e1_ref, e2_ref, e3_ref, w1_ref, w2_ref, kv_ref, both_ref, pair_ref
):
    part, width, slab = e0_ref.shape[0], w1_ref.shape[0], kv_ref.shape[0]
    for k, e_ref in enumerate((e0_ref, e1_ref, e2_ref, e3_ref)):
        start = pl.multiple_of((where_ref[0] ^ k) * part, part)
        pair_ref[pl.ds(start, part), :] = e_ref[...]
    both_ref[:slab, :] = kv_ref[...]
    both_ref[slab:, :width] = mm(pair_ref[...], w1_ref[...], NT).astype(BF)
    both_ref[slab:, width:] = mm(pair_ref[...], w2_ref[...], NT).astype(BF)


def chip_sum(own_ref, other_ref, block, rows):
    near = slice(block * rows, (block + 1) * rows)
    far = slice((block ^ 1) * rows, ((block ^ 1) + 1) * rows)
    return (own_ref[near].astype(F32) + other_ref[far].astype(F32)).astype(BF)


def weights_kernel(xt_ref, xt2_ref, dkv_ref, dkv2_ref, dqo_ref, dqo2_ref, *out_refs):
    kv_refs, keep_ref, send_ref = out_refs[:4], out_refs[4], out_refs[5]
    slab, own = dkv_ref.shape[0] // 4, dqo_ref.shape[0]
    half = dqo_ref.shape[1] // 2
    step = kv_refs[0].shape[0]
    sums = [chip_sum(dkv_ref, dkv2_ref, j, slab) for j in range(4)]
    near = jnp.concatenate([sums[0], sums[2]], axis=0)
    far = jnp.concatenate([sums[1], sums[3]], axis=0)
    for k in (2, 3, 1, 0):
        span = slice(k * step, (k + 1) * step)
        total = mm(xt_ref[span, : 2 * slab], near) + mm(xt2_ref[span, : 2 * slab], far)
        kv_refs[k][...] = total.astype(kv_refs[k].dtype)
        close = slice(k * step // 2, (k + 1) * step // 2)
        for side in (0, 1):
            cols = slice(side * half, (side + 1) * half)
            at = slice(2 * slab + side * own, 2 * slab + (side + 1) * own)
            total = mm(xt_ref[span, at], dqo_ref[:, cols])
            total += mm(xt2_ref[span, at], dqo2_ref[:, cols])
            keep_ref[close, cols] = total[: step // 2]
            send_ref[close, cols] = total[step // 2 :].astype(send_ref.dtype)


def inputs_kernel(dkv_ref, dkv2_ref, pair_ref, dq_ref, wk_ref, wv_ref, wq_ref, out_ref):
    width = wk_ref.shape[0]
    part = pair_ref.shape[0]
    dkv = dkv_ref[:part].astype(F32) + dkv2_ref[part : 2 * part].astype(F32)
    dkv = (dkv + pair_ref[...].astype(F32)).astype(BF)
    rows = out_ref.shape[0] // 4
    for t in range(4):
        span = slice(t * width, (t + 1) * width)
        term = mm(dkv[:, :width], wk_ref[:, span]) + mm(dkv[:, width:], wv_ref[:, span])
        out_ref[t * rows : t * rows + part] = term.astype(BF)
        term = mm(dq_ref[:, :width], wq_ref[:, span])
        out_ref[t * rows + part : (t + 1) * rows] = term.astype(BF)


VMEM = pl.BlockSpec(memory_space=pltpu.VMEM)
SMEM = pl.BlockSpec(memory_space=pltpu.SMEM)


def per_device(query_in, grad_out, encoder_states, frame_lengths, w_query, w_key, w_value, w_out):
    rows_in, rows_grad, frames = query_in[0], grad_out[0], encoder_states[0]
    width = w_query.shape[1]
    heads = width // HD
    model = w_query.shape[0]
    inner = model // 64
    own, slab = rows_in.shape[0], frames.shape[0]
    quarter = slab // 4
    xi, zi, ci, yi = (lax.axis_index(n) for n in ("dp", "z", "core", "head"))
    wq_t, wk_t, wv_t = w_query.T, w_key.T, w_value.T
    where = yi.reshape(1).astype(jnp.int32)

    def call(kernel, outs, ins, scalar=False, scratch=(), work=2):
        shapes = [jax.ShapeDtypeStruct(shape, kind) for shape, kind in outs]
        specs = [SMEM] * scalar + [VMEM] * (len(ins) - scalar)
        return pl.pallas_call(
            kernel,
            out_shape=shapes,
            in_specs=specs,
            out_specs=[VMEM] * len(outs),
            scratch_shapes=scratch,
            compiler_params=pltpu.CompilerParams(vmem_limit_bytes=24 * 1024 * 1024),
            cost_estimate=pl.CostEstimate(
                flops=work, bytes_accessed=0, transcendentals=0
            ),
        )(*ins)

    hbm = pl.BlockSpec(memory_space=pl.ANY)
    weights = [pltpu.VMEM((width, model), BF)] * 4
    rows0, kv, e_part = pl.pallas_call(
        project_kernel,
        out_shape=[
            jax.ShapeDtypeStruct((own, 2 * width), BF),
            jax.ShapeDtypeStruct((slab, 2 * width), BF),
            jax.ShapeDtypeStruct((quarter, model), BF),
        ],
        in_specs=[SMEM] + [hbm] * 7,
        out_specs=[VMEM] * 3,
        scratch_shapes=[pltpu.VMEM((rows, model), BF) for rows in (own, own, slab)]
        + weights
        + [pltpu.SemaphoreType.DMA((12,))],
        compiler_params=pltpu.CompilerParams(vmem_limit_bytes=56 * 1024 * 1024),
    )(where, rows_in, rows_grad, frames, wq_t, w_out, wk_t, wv_t)

    e_part = flip(e_part, "z", 8, 1)
    e_parts = [e_part] + [flip(e_part, "head", 4, k) for k in (1, 2, 3)]

    row_blocks = [rows0] + [flip(rows0, "z", 8, 2 * j) for j in (1, 2, 3)]

    e_parts[1:], row_blocks[1:] = lax.optimization_barrier((e_parts[1:], row_blocks[1:]))
    kv, e_pair = call(
        pair_kernel,
        [((2 * slab, 2 * width), BF), ((slab, model), BF)],
        (where, *e_parts, wk_t, wv_t, kv),
        True,
    )
    both = (kv, swap(kv, "core"))

    def turn(stacked):
        place = jnp.arange(model, dtype=jnp.int32)
        unit, rest = place % inner, place // inner
        a_rel, b_rel = rest % 4, (rest // 4) % 2
        x_rel, c_rel = (rest // 8) % 4, rest // 32
        target = (
            (x_rel ^ xi) * 16 + ((2 * a_rel + b_rel) ^ zi) * 2 + (c_rel ^ ci)
        ) * inner + unit
        pick = (place[:, None] == target[None, :]).astype(BF)
        return mm(pick, stacked, (((0,), (1,)), ((), ()))).astype(BF)

    starts = [
        slab * (2 * (zi ^ db) + (ci ^ dc)) for db in (0, 1) for dc in (0, 1)
    ]
    valid = jnp.stack([frame_lengths[0] - s for s in starts]).astype(jnp.int32)

    (stats,) = call(
        functools.partial(stats_kernel, heads),
        [((16, 4 * own), F32)],
        (valid, *row_blocks, *both),
        True,
    )
    stats, e_pair = lax.optimization_barrier((stats, e_pair))
    all_stats = [stats] + [flip(stats, "z", 8, 2 * j) for j in (1, 2, 3)]

    turned = turn(jnp.concatenate([frames, e_pair, rows_in, rows_grad], axis=0))
    xt, xt_other = turned[: model // 2], swap(turned[model // 2 :], "core")
    all_stats[1:], xt, xt_other = lax.optimization_barrier((all_stats[1:], xt, xt_other))

    dkv, dq0, *dq_sends = call(
        functools.partial(grads_kernel, heads),
        [((4 * slab, 2 * width), BF), ((own, 2 * width), F32)]
        + [((own, 2 * width), BF)] * 3,
        (valid, *row_blocks, *both, *all_stats),
        True,
    )

    dkv_other = swap(dkv, "core")
    dq_recv = [flip(d, "z", 8, 2 * k) for k, d in zip((1, 2, 3), dq_sends)]

    pair = chip_sum(dkv, dkv_other, 2, slab)
    dq_recv, pair = lax.optimization_barrier((dq_recv, pair))
    pair_recv = flip(pair, "z", 8, 1)
    dqo = (dq0 + sum(d.astype(F32) for d in dq_recv)).astype(BF)
    dqo_other, pair_recv = lax.optimization_barrier((swap(dqo, "core"), pair_recv))

    part = model // 8
    kv_own, *kv_sends, qo_keep, qo_send = call(
        weights_kernel,
        [((part, 2 * width), F32)]
        + [((part, 2 * width), BF)] * 3
        + [((2 * part, 2 * width), F32), ((2 * part, 2 * width), BF)],
        (xt, xt_other, dkv, dkv_other, dqo, dqo_other),
    )
    kv_x = [flip(kv_sends[k - 1], "dp", 4, k) for k in (2, 1, 3)]
    qo_b = flip(qo_send, "z", 8, 1)

    dqo, kv_own = lax.optimization_barrier((dqo, kv_own))
    (inputs,) = call(
        inputs_kernel,
        [((4 * (slab + own), width), BF)],
        (dkv, dkv_other, pair_recv, dqo, wk_t, wv_t, wq_t),
    )
    inputs = lax.psum_scatter(inputs, "head", scatter_dimension=0, tiled=True)
    dframes, dinput = inputs[:slab], inputs[slab:]

    cut = part // 2
    kv_sum = kv_own + sum(k.astype(F32) for k in kv_x)
    kv_b = flip(kv_sum[cut:].astype(BF), "z", 8, 1)
    qo_sum = qo_keep + qo_b.astype(F32)
    qo_x = [flip(qo_sum[k * cut : (k + 1) * cut].astype(BF), "dp", 4, k) for k in (2, 1, 3)]
    kv_sum = kv_sum[:cut] + kv_b.astype(F32)
    qo_sum = qo_sum[:cut] + sum(q.astype(F32) for q in qo_x)
    total = jnp.concatenate([kv_sum, qo_sum], axis=1)
    low = total.astype(BF)
    over = [flip(low[k * inner : (k + 1) * inner], "z", 8, 2 * k) for k in (2, 1, 3)]
    total = total[:inner] + sum(p.astype(F32) for p in over)
    return (
        dinput[None],
        dframes[None],
        total[:, 2 * width : 3 * width],
        total[:, :width],
        total[:, width : 2 * width],
        total[:, 3 * width :].T,
    )


def solution(mesh):
    dp, tm, head = mesh.devices.shape
    fine = Mesh(mesh.devices.reshape(dp, tm // 2, 2, head), ("dp", "z", "core", "head"))
    tm = ("z", "core")
    placed = (
        P("dp", tm, None),
        P("dp", tm, None),
        P("dp", tm, None),
        P("dp"),
        P(None, "head"),
        P(None, "head"),
        P(None, "head"),
        P("head", None),
    )
    every = ("dp",) + tm
    return jax.shard_map(
        per_device,
        mesh=fine,
        in_specs=placed,
        out_specs=(
            P("dp", tm, "head"),
            P("dp", tm, "head"),
            P(every, "head"),
            P(every, "head"),
            P(every, "head"),
            P("head", every),
        ),
        check_vma=False,
    )
```

```python
import functools
import math

import jax
import jax.numpy as jnp
from jax import lax
from jax.experimental import pallas as pl
from jax.experimental.pallas import tpu as pltpu
from jax.sharding import Mesh, PartitionSpec as P

HD = 64
BF = jnp.bfloat16
F32 = jnp.float32
SCALE = HD ** (-0.5)
LOG2 = SCALE * math.log2(math.e)
LOW = -1e30
NT = (((1,), (1,)), ((), ()))
TN = (((0,), (0,)), ((), ()))


def mm(left, right, dims=None):
    if dims is None:
        dims = (((1,), (0,)), ((), ()))
    return lax.dot_general(left, right, dims, preferred_element_type=F32)


def flip(x, axis, size, bits):
    return lax.ppermute(x, axis, [(i, i ^ bits) for i in range(size)])


def swap(x, axis):
    return flip(x, axis, 2, 1)


def frame_bias(valid_ref, block, rows):
    positions = lax.broadcasted_iota(jnp.int32, (rows, 1), 0)
    return jnp.where(positions < valid_ref[block], 0.0, LOW)


def stats_kernel(heads, valid_ref, *refs):
    rows_refs, frame_refs, out_ref = refs[:4], refs[4:8], refs[8]
    width = heads * HD
    rows = jnp.concatenate([r[...] for r in rows_refs], axis=0)
    blocks = [r[...] for r in frame_refs]
    biases = [frame_bias(valid_ref, j, b.shape[0]) for j, b in enumerate(blocks)]
    out_ref[...] = jnp.zeros_like(out_ref)
    for h in range(heads):
        cut = slice(h * HD, (h + 1) * HD)
        cut2 = slice(width + h * HD, width + (h + 1) * HD)
        query, dout = rows[:, cut], rows[:, cut2]
        scores = [
            mm(b[:, cut], query, NT) * LOG2 + bias for b, bias in zip(blocks, biases)
        ]
        top = functools.reduce(
            jnp.maximum, [jnp.max(s, axis=0, keepdims=True) for s in scores]
        )
        top = jnp.maximum(top, 0.1 * LOW)
        total = jnp.zeros_like(top)
        delta = jnp.zeros_like(top)
        for s, b in zip(scores, blocks):
            weight = jnp.exp2(s - top)
            dprobs = mm(b[:, cut2], dout, NT)
            total += jnp.sum(weight, axis=0, keepdims=True)
            delta += jnp.sum(weight * dprobs, axis=0, keepdims=True)
        total = jnp.maximum(total, 1.0)
        out_ref[h : h + 1, :] = top + jnp.log2(total)
        out_ref[8 + h : 9 + h, :] = delta / total


def in_own_order(x, k, own):
    if k & 2:
        x = pltpu.roll(x, 2 * own, 1)
    if k & 1:
        lane = lax.broadcasted_iota(jnp.int32, x.shape, 1)
        x = jnp.where(
            lane % (2 * own) < own, pltpu.roll(x, 3 * own, 1), pltpu.roll(x, own, 1)
        )
    return x


def grads_kernel(heads, valid_ref, *refs):
    rows_refs, frame_refs, stat_refs = refs[:4], refs[4:8], refs[8:12]
    keep_refs, send_ref = refs[12:14], refs[14]
    dq_refs = refs[15:19]
    width = heads * HD
    rows = jnp.concatenate([r[...] for r in rows_refs], axis=0)
    blocks = [r[...] for r in frame_refs]
    part = blocks[0].shape[0]
    own = rows_refs[0].shape[0]
    stats = [in_own_order(stat_refs[k][...], k, own) for k in range(4)]
    tops = [s[:8] for s in stats]
    top = functools.reduce(jnp.maximum, tops)
    shares = [jnp.exp2(t - top) for t in tops]
    total = functools.reduce(jnp.add, shares)
    lse = top + jnp.log2(total)
    delta = functools.reduce(
        jnp.add, [w * s[8:] for w, s in zip(shares, stats)]
    ) / total
    biases = [frame_bias(valid_ref, j, part) for j in range(4)]
    dq_t, att_t = [], []
    for h in range(heads):
        cut = slice(h * HD, (h + 1) * HD)
        cut2 = slice(width + h * HD, width + (h + 1) * HD)
        query, dout = rows[:, cut], rows[:, cut2]
        dq_sum = jnp.zeros((HD, rows.shape[0]), F32)
        att_sum = jnp.zeros((HD, rows.shape[0]), F32)
        for j, (b, bias) in enumerate(zip(blocks, biases)):
            key, value = b[:, cut], b[:, cut2]
            scores = mm(key, query, NT) * LOG2 + bias
            probs = jnp.exp2(scores - lse[h : h + 1])
            dprobs = mm(value, dout, NT)
            dscores = (probs * (dprobs - delta[h : h + 1])).astype(BF)
            probs = probs.astype(BF)
            dkey = mm(dscores, query) * SCALE
            dvalue = mm(probs, dout)
            out_ref = send_ref if j % 2 else keep_refs[j // 2]
            span = slice((j // 2) * part, (j // 2 + 1) * part) if j % 2 else slice(0, part)
            out_ref[span, cut] = dkey.astype(out_ref.dtype)
            out_ref[span, cut2] = dvalue.astype(out_ref.dtype)
            dq_sum += mm(key, dscores, TN)
            att_sum += mm(value, probs, TN)
        dq_t.append(dq_sum * SCALE)
        att_t.append(att_sum)
    joined = jnp.concatenate(dq_t + att_t, axis=0).T
    for k in range(4):
        dq_refs[k][...] = joined[k * own : (k + 1) * own].astype(dq_refs[k].dtype)


QUAD = (0, 2, 5, 7)


def fetch(pairs, sems):
    copies = [
        pltpu.make_async_copy(source, target, sems.at[i])
        for i, (source, target) in enumerate(pairs)
    ]
    for copy in copies:
        copy.start()
    return copies


def project_kernel(
    left_ref, right_ref, frames_ref, wq_ref, wo_ref, wk_ref, wv_ref, rows_ref, kv_ref,
    left, right, frames, wq, wo, wk, wv, sems,
):
    width = wq.shape[0]
    half = width // 2
    pairs = [(left_ref, left)]
    for source, target in ((wq_ref, wq), (wo_ref, wo), (wk_ref, wk), (wv_ref, wv)):
        pairs += [
            (source.at[:half], target.at[:half]),
            (source.at[half:], target.at[half:]),
        ]
        if source is wq_ref:
            pairs.append((right_ref, right))
        if source is wo_ref:
            pairs.append((frames_ref, frames))
    copies = fetch(pairs, sems)
    for i, (x, w, out, side) in enumerate(
        ((left, wq, rows_ref, 0), (right, wo, rows_ref, 1), (frames, wk, kv_ref, 0), (frames, wv, kv_ref, 1))
    ):
        for copy in copies[3 * i : 3 * i + 3]:
            copy.wait()
        out[:, side * width : (side + 1) * width] = mm(x[...], w[...], NT).astype(BF)


def collect_kernel(keep_ref, core_ref, pair_ref, dq_ref, a_ref, b_ref, c_ref, out_ref):
    slab = keep_ref.shape[0]
    total = keep_ref[...] + core_ref[:slab].astype(F32) + pair_ref[...].astype(F32)
    out_ref[:slab] = total.astype(out_ref.dtype)
    total = dq_ref[...] + a_ref[...].astype(F32) + b_ref[...].astype(F32)
    out_ref[slab:] = (total + c_ref[...].astype(F32)).astype(out_ref.dtype)


def weights_kernel(part, xt_ref, xt2_ref, y_ref, y2_ref, *out_refs):
    kv_refs, keep_ref, send_ref = out_refs[:4], out_refs[4], out_refs[5]
    frames = y_ref.shape[0] - part
    half = y_ref.shape[1] // 2
    step = kv_refs[0].shape[0]
    pairs = ((xt_ref, y_ref), (xt2_ref, y2_ref))
    for k in (3, 1, 2, 0):
        span = slice(k * step, (k + 1) * step)
        kv = sum(mm(x[span, :frames], y[:frames, :]) for x, y in pairs)
        kv_refs[k][...] = kv.astype(kv_refs[k].dtype)
        q = sum(
            mm(x[span, frames : frames + part], y[frames:, :half]) for x, y in pairs
        )
        o = sum(mm(x[span, frames + part :], y[frames:, half:]) for x, y in pairs)
        near = slice(k * step // 2, (k + 1) * step // 2)
        keep_ref[near, :half] = q[: step // 2]
        keep_ref[near, half:] = o[: step // 2]
        send_ref[near, :half] = q[step // 2 :].astype(send_ref.dtype)
        send_ref[near, half:] = o[step // 2 :].astype(send_ref.dtype)


def inputs_kernel(where_ref, y_ref, wk_ref, wv_ref, wq_ref, own_ref, *refs):
    send_refs, (scratch, wk, wv, wq, sems) = refs[:3], refs[3:]
    width = wk.shape[0]
    half = width // 2
    pairs = []
    for source, target in ((wk_ref, wk), (wv_ref, wv), (wq_ref, wq)):
        pairs += [
            (source.at[:half], target.at[:half]),
            (source.at[half:], target.at[half:]),
        ]
    copies = fetch(pairs, sems)
    part = y_ref.shape[0] // 5 * 4
    dkey, dvalue = y_ref[:part, :width], y_ref[:part, width:]
    dquery = y_ref[part:, :width]
    for copy in copies:
        copy.wait()
    for t in range(4):
        span = slice(t * width, (t + 1) * width)
        scratch[t, :part] = mm(dkey, wk[:, span]) + mm(dvalue, wv[:, span])
        scratch[t, part:] = mm(dquery, wq[:, span])
    own_ref[...] = scratch[where_ref[0]]
    for k in (1, 2, 3):
        send_refs[k - 1][...] = scratch[where_ref[0] ^ k].astype(BF)


VMEM = pl.BlockSpec(memory_space=pltpu.VMEM)
SMEM = pl.BlockSpec(memory_space=pltpu.SMEM)


def per_device(query_in, grad_out, encoder_states, frame_lengths, w_query, w_key, w_value, w_out):
    rows_in, rows_grad, frames = query_in[0], grad_out[0], encoder_states[0]
    width = w_query.shape[1]
    heads = width // HD
    model = w_query.shape[0]
    inner = model // 64
    own, slab = rows_in.shape[0], frames.shape[0]
    quarter = slab // 4
    xi, zi, ci, yi = (lax.axis_index(n) for n in ("dp", "z", "core", "head"))
    wq_t, wk_t, wv_t = w_query.T, w_key.T, w_value.T
    where = yi.reshape(1).astype(jnp.int32)

    def call(kernel, outs, ins, scalar=False, scratch=(), work=2):
        shapes = [jax.ShapeDtypeStruct(shape, kind) for shape, kind in outs]
        specs = [SMEM] * scalar + [VMEM] * (len(ins) - scalar)
        return pl.pallas_call(
            kernel,
            out_shape=shapes,
            in_specs=specs,
            out_specs=[VMEM] * len(outs),
            scratch_shapes=scratch,
            compiler_params=pltpu.CompilerParams(vmem_limit_bytes=24 * 1024 * 1024),
            cost_estimate=pl.CostEstimate(
                flops=work, bytes_accessed=0, transcendentals=0
            ),
        )(*ins)

    hbm = pl.BlockSpec(memory_space=pl.ANY)
    weights = [pltpu.VMEM((width, model), BF)] * 4
    rows0, kv = pl.pallas_call(
        project_kernel,
        out_shape=[
            jax.ShapeDtypeStruct((own, 2 * width), BF),
            jax.ShapeDtypeStruct((slab, 2 * width), BF),
        ],
        in_specs=[hbm] * 7,
        out_specs=[VMEM] * 2,
        scratch_shapes=[pltpu.VMEM((rows, model), BF) for rows in (own, own, slab)]
        + weights
        + [pltpu.SemaphoreType.DMA((12,))],
        compiler_params=pltpu.CompilerParams(vmem_limit_bytes=56 * 1024 * 1024),
    )(rows_in, rows_grad, frames, wq_t, w_out, wk_t, wv_t)

    kv_pair = flip(kv, "z", 8, 1)
    kv_core = swap(kv, "core")
    rows0, kv_core = lax.optimization_barrier((rows0, kv_core))
    row_blocks = [rows0] + [flip(rows0, "z", 8, QUAD[j]) for j in (1, 2, 3)]

    def turn(stacked, c_rel):
        place = jnp.arange(model // 2, dtype=jnp.int32)
        unit, rest = place % inner, place // inner
        a_rel, b_rel = rest % 4, (rest // 4) % 2
        x_rel = rest // 8
        target = (
            (x_rel ^ xi) * 16 + ((2 * (a_rel % 2)) ^ (5 * (a_rel // 2)) ^ b_rel ^ zi) * 2 + (c_rel ^ ci)
        ) * inner + unit
        pick = (jnp.arange(model, dtype=jnp.int32)[None, :] == target[:, None]).astype(BF)
        return mm(pick, stacked, NT).astype(BF)

    stacked = jnp.concatenate([frames, rows_in, rows_grad], axis=0)
    xt, xt_send = turn(stacked, 0), turn(stacked, 1)
    row_blocks[1:], kv_pair, kv_core, xt, xt_send = lax.optimization_barrier(
        (row_blocks[1:], kv_pair, kv_core, xt, xt_send)
    )
    xt_other = swap(xt_send, "core")
    frame_blocks = [kv, kv_core, kv_pair, swap(kv_pair, "core")]
    starts = [
        slab * (2 * (zi ^ db) + (ci ^ dc)) for db in (0, 1) for dc in (0, 1)
    ]
    valid = jnp.stack([frame_lengths[0] - s for s in starts]).astype(jnp.int32)

    (stats,) = call(
        functools.partial(stats_kernel, heads),
        [((16, 4 * own), F32)],
        (valid, *row_blocks, *frame_blocks),
        True,
    )
    all_stats = [stats] + [flip(stats, "z", 8, QUAD[j]) for j in (1, 2, 3)]

    all_stats[1:], xt_other = lax.optimization_barrier((all_stats[1:], xt_other))

    keep0, keep1, send, dq0, *dq_sends = call(
        functools.partial(grads_kernel, heads),
        [((slab, 2 * width), F32)] * 2
        + [((2 * slab, 2 * width), BF), ((own, 2 * width), F32)]
        + [((own, 2 * width), BF)] * 3,
        (valid, *row_blocks, *frame_blocks, *all_stats),
        True,
    )

    recv = swap(send, "core")
    pair = (keep1 + recv[slab:].astype(F32)).astype(BF)
    dq_sends, pair = lax.optimization_barrier((dq_sends, pair))
    pair_recv = flip(pair, "z", 8, 1)
    dq_recv = [flip(d, "z", 8, QUAD[k]) for k, d in zip((1, 2, 3), dq_sends)]
    (grads,) = call(
        collect_kernel,
        [((slab + own, 2 * width), BF)],
        (keep0, recv, pair_recv, dq0, *dq_recv),
    )
    grads_other = swap(grads, "core")

    part = model // 8
    kv_own, *kv_sends, qo_keep, qo_send = call(
        functools.partial(weights_kernel, own),
        [((part, 2 * width), F32)]
        + [((part, 2 * width), BF)] * 3
        + [((2 * part, 2 * width), F32), ((2 * part, 2 * width), BF)],
        (xt, xt_other, grads, grads_other),
    )
    kv_x = [flip(kv_sends[k - 1], "dp", 4, k) for k in (2, 1, 3)]
    qo_b = flip(qo_send, "z", 8, 1)

    held, kv_own = lax.optimization_barrier((grads, kv_own))
    own_part, *sends = pl.pallas_call(
        inputs_kernel,
        out_shape=[jax.ShapeDtypeStruct((slab + own, width), F32)]
        + [jax.ShapeDtypeStruct((slab + own, width), BF)] * 3,
        in_specs=[SMEM, VMEM] + [pl.BlockSpec(memory_space=pltpu.HBM)] * 3,
        out_specs=[VMEM] * 4,
        scratch_shapes=[pltpu.VMEM((4, slab + own, width), F32)]
        + weights[:3]
        + [pltpu.SemaphoreType.DMA((6,))],
        compiler_params=pltpu.CompilerParams(vmem_limit_bytes=24 * 1024 * 1024),
        cost_estimate=pl.CostEstimate(
            flops=12_000_000_000, bytes_accessed=0, transcendentals=0
        ),
    )(where, held, wk_t, wv_t, wq_t)
    arrived = [flip(sends[k - 1], "head", 4, k) for k in (2, 1, 3)]
    inputs = (own_part + sum(p.astype(F32) for p in arrived)).astype(BF)
    dframes, dinput = inputs[:slab], inputs[slab:]

    cut = part // 2
    kv_sum = kv_own + sum(k.astype(F32) for k in kv_x)
    kv_b = flip(kv_sum[cut:].astype(BF), "z", 8, 1)
    qo_sum = qo_keep + qo_b.astype(F32)
    qo_x = [flip(qo_sum[k * cut : (k + 1) * cut].astype(BF), "dp", 4, k) for k in (2, 1, 3)]
    kv_sum = kv_sum[:cut] + kv_b.astype(F32)
    qo_sum = qo_sum[:cut] + sum(q.astype(F32) for q in qo_x)
    total = jnp.concatenate([kv_sum, qo_sum], axis=1)
    low = total.astype(BF)
    over = [flip(low[k * inner : (k + 1) * inner], "z", 8, QUAD[k]) for k in (2, 1, 3)]
    total = total[:inner] + sum(p.astype(F32) for p in over)
    return (
        dinput[None],
        dframes[None],
        total[:, 2 * width : 3 * width],
        total[:, :width],
        total[:, width : 2 * width],
        total[:, 3 * width :].T,
    )


def solution(mesh):
    dp, tm, head = mesh.devices.shape
    fine = Mesh(mesh.devices.reshape(dp, tm // 2, 2, head), ("dp", "z", "core", "head"))
    tm = ("z", "core")
    placed = (
        P("dp", tm, None),
        P("dp", tm, None),
        P("dp", tm, None),
        P("dp"),
        P(None, "head"),
        P(None, "head"),
        P(None, "head"),
        P("head", None),
    )
    every = ("dp",) + tm
    return jax.shard_map(
        per_device,
        mesh=fine,
        in_specs=placed,
        out_specs=(
            P("dp", tm, "head"),
            P("dp", tm, "head"),
            P(every, "head"),
            P(every, "head"),
            P(every, "head"),
            P("head", every),
        ),
        check_vma=False,
    )
```

```python
import functools
import math

import jax
import jax.numpy as jnp
from jax import lax
from jax.experimental import pallas as pl
from jax.experimental.pallas import tpu as pltpu
from jax.sharding import Mesh, PartitionSpec as P

HD = 64
BF = jnp.bfloat16
F32 = jnp.float32
SCALE = HD ** (-0.5)
LOG2 = SCALE * math.log2(math.e)
LOW = -1e30
NT = (((1,), (1,)), ((), ()))
TN = (((0,), (0,)), ((), ()))


def mm(left, right, dims=None):
    if dims is None:
        dims = (((1,), (0,)), ((), ()))
    return lax.dot_general(left, right, dims, preferred_element_type=F32)


def flip(x, axis, size, bits):
    return lax.ppermute(x, axis, [(i, i ^ bits) for i in range(size)])


def swap(x, axis):
    return flip(x, axis, 2, 1)


def frame_bias(valid_ref, block, rows):
    positions = lax.broadcasted_iota(jnp.int32, (rows, 1), 0)
    return jnp.where(positions < valid_ref[block], 0.0, LOW)


SPAN = 2


def joined_blocks(valid_ref, refs, span):
    blocks, biases = [], []
    for first in range(0, len(refs), span):
        some = range(first, first + span)
        blocks.append(jnp.concatenate([refs[j][...] for j in some], axis=0))
        biases.append(
            jnp.concatenate([frame_bias(valid_ref, j, refs[j].shape[0]) for j in some], axis=0)
        )
    return blocks, biases


def stats_kernel(heads, valid_ref, *refs):
    rows_refs, frame_refs, out_ref = refs[:4], refs[4:8], refs[8]
    width = heads * HD
    rows = jnp.concatenate([r[...] for r in rows_refs], axis=0)
    blocks, biases = joined_blocks(valid_ref, frame_refs, 1)
    out_ref[...] = jnp.zeros_like(out_ref)
    for h in range(heads):
        cut = slice(h * HD, (h + 1) * HD)
        cut2 = slice(width + h * HD, width + (h + 1) * HD)
        query, dout = rows[:, cut], rows[:, cut2]
        scores = [
            mm(b[:, cut], query, NT) * LOG2 + bias for b, bias in zip(blocks, biases)
        ]
        top = functools.reduce(
            jnp.maximum, [jnp.max(s, axis=0, keepdims=True) for s in scores]
        )
        top = jnp.maximum(top, 0.1 * LOW)
        total = jnp.zeros_like(top)
        delta = jnp.zeros_like(top)
        for s, b in zip(scores, blocks):
            weight = jnp.exp2(s - top)
            dprobs = mm(b[:, cut2], dout, NT)
            total += jnp.sum(weight, axis=0, keepdims=True)
            delta += jnp.sum(weight * dprobs, axis=0, keepdims=True)
        total = jnp.maximum(total, 1.0)
        out_ref[h : h + 1, :] = top + jnp.log2(total)
        out_ref[8 + h : 9 + h, :] = delta / total


def in_own_order(x, k, own):
    if k & 2:
        x = pltpu.roll(x, 2 * own, 1)
    if k & 1:
        lane = lax.broadcasted_iota(jnp.int32, x.shape, 1)
        x = jnp.where(
            lane % (2 * own) < own, pltpu.roll(x, 3 * own, 1), pltpu.roll(x, own, 1)
        )
    return x


def grads_kernel(heads, valid_ref, *refs):
    rows_refs, frame_refs, stat_refs = refs[:4], refs[4:8], refs[8:12]
    keep_refs, send_ref = refs[12:14], refs[14]
    dq_refs = refs[15:19]
    width = heads * HD
    rows = jnp.concatenate([r[...] for r in rows_refs], axis=0)
    blocks, biases = joined_blocks(valid_ref, frame_refs, SPAN)
    part = frame_refs[0].shape[0]
    own = rows_refs[0].shape[0]
    stats = [in_own_order(stat_refs[k][...], k, own) for k in range(4)]
    tops = [s[:8] for s in stats]
    top = functools.reduce(jnp.maximum, tops)
    shares = [jnp.exp2(t - top) for t in tops]
    total = functools.reduce(jnp.add, shares)
    lse = top + jnp.log2(total)
    delta = functools.reduce(
        jnp.add, [w * s[8:] for w, s in zip(shares, stats)]
    ) / total
    dq_t, att_t = [], []
    for h in range(heads):
        cut = slice(h * HD, (h + 1) * HD)
        cut2 = slice(width + h * HD, width + (h + 1) * HD)
        query, dout = rows[:, cut], rows[:, cut2]
        dq_sum = jnp.zeros((HD, rows.shape[0]), F32)
        att_sum = jnp.zeros((HD, rows.shape[0]), F32)
        for j, (b, bias) in enumerate(zip(blocks, biases)):
            key, value = b[:, cut], b[:, cut2]
            scores = mm(key, query, NT) * LOG2 + bias
            probs = jnp.exp2(scores - lse[h : h + 1])
            dprobs = mm(value, dout, NT)
            dscores = (probs * (dprobs - delta[h : h + 1])).astype(BF)
            probs = probs.astype(BF)
            dkey = mm(dscores, query) * SCALE
            dvalue = mm(probs, dout)
            for i in range(SPAN):
                owner, at = j * SPAN + i, slice(i * part, (i + 1) * part)
                out_ref = send_ref if owner % 2 else keep_refs[owner // 2]
                low = (owner // 2) * part if owner % 2 else 0
                out_ref[low : low + part, cut] = dkey[at].astype(out_ref.dtype)
                out_ref[low : low + part, cut2] = dvalue[at].astype(out_ref.dtype)
            dq_sum += mm(key, dscores, TN)
            att_sum += mm(value, probs, TN)
        dq_t.append(dq_sum * SCALE)
        att_t.append(att_sum)
    joined = jnp.concatenate(dq_t + att_t, axis=0).T
    for k in range(4):
        dq_refs[k][...] = joined[k * own : (k + 1) * own].astype(dq_refs[k].dtype)


QUAD = (0, 2, 5, 7)


def fetch(pairs, sems):
    copies = [
        pltpu.make_async_copy(source, target, sems.at[i])
        for i, (source, target) in enumerate(pairs)
    ]
    for copy in copies:
        copy.start()
    return copies


def project_kernel(
    left_ref, right_ref, frames_ref, wq_ref, wo_ref, wk_ref, wv_ref, rows_ref, kv_ref,
    left, right, frames, wq, wo, wk, wv, sems,
):
    width = wq.shape[0]
    half = width // 2
    pairs = [(left_ref, left)]
    for source, target in ((wq_ref, wq), (wo_ref, wo), (wk_ref, wk), (wv_ref, wv)):
        pairs += [
            (source.at[:half], target.at[:half]),
            (source.at[half:], target.at[half:]),
        ]
        if source is wq_ref:
            pairs.append((right_ref, right))
        if source is wo_ref:
            pairs.append((frames_ref, frames))
    copies = fetch(pairs, sems)
    for i, (x, w, out, side) in enumerate(
        ((left, wq, rows_ref, 0), (right, wo, rows_ref, 1), (frames, wk, kv_ref, 0), (frames, wv, kv_ref, 1))
    ):
        for copy in copies[3 * i : 3 * i + 3]:
            copy.wait()
        out[:, side * width : (side + 1) * width] = mm(x[...], w[...], NT).astype(BF)


def collect_kernel(keep_ref, core_ref, pair_ref, dq_ref, a_ref, b_ref, c_ref, out_ref):
    slab = keep_ref.shape[0]
    total = keep_ref[...] + core_ref[:slab].astype(F32) + pair_ref[...].astype(F32)
    out_ref[:slab] = total.astype(out_ref.dtype)
    total = dq_ref[...] + a_ref[...].astype(F32) + b_ref[...].astype(F32)
    out_ref[slab:] = (total + c_ref[...].astype(F32)).astype(out_ref.dtype)


def weights_kernel(part, xt_ref, xt2_ref, y_ref, y2_ref, *out_refs):
    kv_refs, keep_ref, send_ref = out_refs[:4], out_refs[4], out_refs[5]
    frames = y_ref.shape[0] - part
    half = y_ref.shape[1] // 2
    step = kv_refs[0].shape[0]
    pairs = ((xt_ref, y_ref), (xt2_ref, y2_ref))
    for k in (3, 1, 2, 0):
        span = slice(k * step, (k + 1) * step)
        kv = sum(mm(x[span, :frames], y[:frames, :]) for x, y in pairs)
        kv_refs[k][...] = kv.astype(kv_refs[k].dtype)
        q = sum(
            mm(x[span, frames : frames + part], y[frames:, :half]) for x, y in pairs
        )
        o = sum(mm(x[span, frames + part :], y[frames:, half:]) for x, y in pairs)
        near = slice(k * step // 2, (k + 1) * step // 2)
        keep_ref[near, :half] = q[: step // 2]
        keep_ref[near, half:] = o[: step // 2]
        send_ref[near, :half] = q[step // 2 :].astype(send_ref.dtype)
        send_ref[near, half:] = o[step // 2 :].astype(send_ref.dtype)


def inputs_kernel(where_ref, y_ref, wk_ref, wv_ref, wq_ref, own_ref, *refs):
    send_refs, (scratch, wk, wv, wq, sems) = refs[:3], refs[3:]
    width = wk.shape[0]
    half = width // 2
    pairs = []
    for source, target in ((wk_ref, wk), (wv_ref, wv), (wq_ref, wq)):
        pairs += [
            (source.at[:half], target.at[:half]),
            (source.at[half:], target.at[half:]),
        ]
    copies = fetch(pairs, sems)
    part = y_ref.shape[0] // 5 * 4
    dkey, dvalue = y_ref[:part, :width], y_ref[:part, width:]
    dquery = y_ref[part:, :width]
    for copy in copies:
        copy.wait()
    for t in range(4):
        span = slice(t * width, (t + 1) * width)
        scratch[t, :part] = mm(dkey, wk[:, span]) + mm(dvalue, wv[:, span])
        scratch[t, part:] = mm(dquery, wq[:, span])
    own_ref[...] = scratch[where_ref[0]]
    for k in (1, 2, 3):
        send_refs[k - 1][...] = scratch[where_ref[0] ^ k].astype(BF)


VMEM = pl.BlockSpec(memory_space=pltpu.VMEM)
SMEM = pl.BlockSpec(memory_space=pltpu.SMEM)


def per_device(query_in, grad_out, encoder_states, frame_lengths, w_query, w_key, w_value, w_out):
    rows_in, rows_grad, frames = query_in[0], grad_out[0], encoder_states[0]
    width = w_query.shape[1]
    heads = width // HD
    model = w_query.shape[0]
    inner = model // 64
    own, slab = rows_in.shape[0], frames.shape[0]
    quarter = slab // 4
    xi, zi, ci, yi = (lax.axis_index(n) for n in ("dp", "z", "core", "head"))
    wq_t, wk_t, wv_t = w_query.T, w_key.T, w_value.T
    where = yi.reshape(1).astype(jnp.int32)

    def call(kernel, outs, ins, scalar=False, scratch=(), work=2):
        shapes = [jax.ShapeDtypeStruct(shape, kind) for shape, kind in outs]
        specs = [SMEM] * scalar + [VMEM] * (len(ins) - scalar)
        return pl.pallas_call(
            kernel,
            out_shape=shapes,
            in_specs=specs,
            out_specs=[VMEM] * len(outs),
            scratch_shapes=scratch,
            compiler_params=pltpu.CompilerParams(vmem_limit_bytes=24 * 1024 * 1024),
            cost_estimate=pl.CostEstimate(
                flops=work, bytes_accessed=0, transcendentals=0
            ),
        )(*ins)

    hbm = pl.BlockSpec(memory_space=pl.ANY)
    weights = [pltpu.VMEM((width, model), BF)] * 4
    rows0, kv = pl.pallas_call(
        project_kernel,
        out_shape=[
            jax.ShapeDtypeStruct((own, 2 * width), BF),
            jax.ShapeDtypeStruct((slab, 2 * width), BF),
        ],
        in_specs=[hbm] * 7,
        out_specs=[VMEM] * 2,
        scratch_shapes=[pltpu.VMEM((rows, model), BF) for rows in (own, own, slab)]
        + weights
        + [pltpu.SemaphoreType.DMA((12,))],
        compiler_params=pltpu.CompilerParams(vmem_limit_bytes=56 * 1024 * 1024),
    )(rows_in, rows_grad, frames, wq_t, w_out, wk_t, wv_t)

    kv_pair = flip(kv, "z", 8, 1)
    kv_core = swap(kv, "core")
    rows0, kv_core = lax.optimization_barrier((rows0, kv_core))
    row_blocks = [rows0] + [flip(rows0, "z", 8, QUAD[j]) for j in (1, 2, 3)]

    def turn(stacked, c_rel):
        place = jnp.arange(model // 2, dtype=jnp.int32)
        unit, rest = place % inner, place // inner
        a_rel, b_rel = rest % 4, (rest // 4) % 2
        x_rel = rest // 8
        target = (
            (x_rel ^ xi) * 16 + ((2 * (a_rel % 2)) ^ (5 * (a_rel // 2)) ^ b_rel ^ zi) * 2 + (c_rel ^ ci)
        ) * inner + unit
        pick = (jnp.arange(model, dtype=jnp.int32)[None, :] == target[:, None]).astype(BF)
        return mm(pick, stacked, NT).astype(BF)

    stacked = jnp.concatenate([frames, rows_in, rows_grad], axis=0)
    xt, xt_send = turn(stacked, 0), turn(stacked, 1)
    row_blocks[1:], kv_pair, kv_core, xt, xt_send = lax.optimization_barrier(
        (row_blocks[1:], kv_pair, kv_core, xt, xt_send)
    )
    xt_other = swap(xt_send, "core")
    frame_blocks = [kv, kv_core, kv_pair, swap(kv_pair, "core")]
    starts = [
        slab * (2 * (zi ^ db) + (ci ^ dc)) for db in (0, 1) for dc in (0, 1)
    ]
    valid = jnp.stack([frame_lengths[0] - s for s in starts]).astype(jnp.int32)

    (stats,) = call(
        functools.partial(stats_kernel, heads),
        [((16, 4 * own), F32)],
        (valid, *row_blocks, *frame_blocks),
        True,
    )
    all_stats = [stats] + [flip(stats, "z", 8, QUAD[j]) for j in (1, 2, 3)]

    all_stats[1:], xt_other = lax.optimization_barrier((all_stats[1:], xt_other))

    keep0, keep1, send, dq0, *dq_sends = call(
        functools.partial(grads_kernel, heads),
        [((slab, 2 * width), F32)] * 2
        + [((2 * slab, 2 * width), BF), ((own, 2 * width), F32)]
        + [((own, 2 * width), BF)] * 3,
        (valid, *row_blocks, *frame_blocks, *all_stats),
        True,
    )

    recv = swap(send, "core")
    pair = (keep1 + recv[slab:].astype(F32)).astype(BF)
    dq_sends, pair = lax.optimization_barrier((dq_sends, pair))
    pair_recv = flip(pair, "z", 8, 1)
    dq_recv = [flip(d, "z", 8, QUAD[k]) for k, d in zip((1, 2, 3), dq_sends)]
    (grads,) = call(
        collect_kernel,
        [((slab + own, 2 * width), BF)],
        (keep0, recv, pair_recv, dq0, *dq_recv),
    )
    grads_other = swap(grads, "core")

    part = model // 8
    kv_own, *kv_sends, qo_keep, qo_send = call(
        functools.partial(weights_kernel, own),
        [((part, 2 * width), F32)]
        + [((part, 2 * width), BF)] * 3
        + [((2 * part, 2 * width), F32), ((2 * part, 2 * width), BF)],
        (xt, xt_other, grads, grads_other),
    )
    kv_x = [flip(kv_sends[k - 1], "dp", 4, k) for k in (2, 1, 3)]
    qo_b = flip(qo_send, "z", 8, 1)

    held, kv_own = lax.optimization_barrier((grads, kv_own))
    own_part, *sends = pl.pallas_call(
        inputs_kernel,
        out_shape=[jax.ShapeDtypeStruct((slab + own, width), F32)]
        + [jax.ShapeDtypeStruct((slab + own, width), BF)] * 3,
        in_specs=[SMEM, VMEM] + [pl.BlockSpec(memory_space=pltpu.HBM)] * 3,
        out_specs=[VMEM] * 4,
        scratch_shapes=[pltpu.VMEM((4, slab + own, width), F32)]
        + weights[:3]
        + [pltpu.SemaphoreType.DMA((6,))],
        compiler_params=pltpu.CompilerParams(vmem_limit_bytes=24 * 1024 * 1024),
        cost_estimate=pl.CostEstimate(
            flops=12_000_000_000, bytes_accessed=0, transcendentals=0
        ),
    )(where, held, wk_t, wv_t, wq_t)
    arrived = [flip(sends[k - 1], "head", 4, k) for k in (2, 1)]

    cut = part // 2
    kv_sum = kv_own + sum(k.astype(F32) for k in kv_x)
    kv_b = flip(kv_sum[cut:].astype(BF), "z", 8, 1)
    qo_sum = qo_keep + qo_b.astype(F32)
    qo_x = [flip(qo_sum[k * cut : (k + 1) * cut].astype(BF), "dp", 4, k) for k in (2, 1, 3)]
    kv_sum = kv_sum[:cut] + kv_b.astype(F32)
    qo_sum = qo_sum[:cut] + sum(q.astype(F32) for q in qo_x)
    total = jnp.concatenate([kv_sum, qo_sum], axis=1)
    total, sends[2], arrived = lax.optimization_barrier((total, sends[2], arrived))
    arrived.append(flip(sends[2], "head", 4, 3))
    low = total.astype(BF)
    over = [flip(low[k * inner : (k + 1) * inner], "z", 8, QUAD[k]) for k in (2, 1, 3)]
    total = total[:inner] + sum(p.astype(F32) for p in over)
    inputs = (own_part + sum(p.astype(F32) for p in arrived)).astype(BF)
    dframes, dinput = inputs[:slab], inputs[slab:]
    return (
        dinput[None],
        dframes[None],
        total[:, 2 * width : 3 * width],
        total[:, :width],
        total[:, width : 2 * width],
        total[:, 3 * width :].T,
    )


def solution(mesh):
    dp, tm, head = mesh.devices.shape
    fine = Mesh(mesh.devices.reshape(dp, tm // 2, 2, head), ("dp", "z", "core", "head"))
    tm = ("z", "core")
    placed = (
        P("dp", tm, None),
        P("dp", tm, None),
        P("dp", tm, None),
        P("dp"),
        P(None, "head"),
        P(None, "head"),
        P(None, "head"),
        P("head", None),
    )
    every = ("dp",) + tm
    return jax.shard_map(
        per_device,
        mesh=fine,
        in_specs=placed,
        out_specs=(
            P("dp", tm, "head"),
            P("dp", tm, "head"),
            P(every, "head"),
            P(every, "head"),
            P(every, "head"),
            P("head", every),
        ),
        check_vma=False,
    )
```

```python
import functools
import math

import jax
import jax.numpy as jnp
from jax import lax
from jax.experimental import pallas as pl
from jax.experimental.pallas import tpu as pltpu
from jax.sharding import Mesh, PartitionSpec as P

HD = 64
BF = jnp.bfloat16
F32 = jnp.float32
SCALE = HD ** (-0.5)
LOG2 = SCALE * math.log2(math.e)
LOW = -1e30
NT = (((1,), (1,)), ((), ()))
TN = (((0,), (0,)), ((), ()))


def mm(left, right, dims=None):
    if dims is None:
        dims = (((1,), (0,)), ((), ()))
    return lax.dot_general(left, right, dims, preferred_element_type=F32)


def flip(x, axis, size, bits):
    return lax.ppermute(x, axis, [(i, i ^ bits) for i in range(size)])


def swap(x, axis):
    return flip(x, axis, 2, 1)


def frame_bias(valid_ref, block, rows):
    positions = lax.broadcasted_iota(jnp.int32, (rows, 1), 0)
    return jnp.where(positions < valid_ref[block], 0.0, LOW)


SPAN = 2


def joined_blocks(valid_ref, refs, span):
    blocks, biases = [], []
    for first in range(0, len(refs), span):
        some = range(first, first + span)
        blocks.append(jnp.concatenate([refs[j][...] for j in some], axis=0))
        biases.append(
            jnp.concatenate([frame_bias(valid_ref, j, refs[j].shape[0]) for j in some], axis=0)
        )
    return blocks, biases


def stats_kernel(heads, valid_ref, *refs):
    rows_refs, frame_refs, out_ref = refs[:4], refs[4:8], refs[8]
    width = heads * HD
    rows = jnp.concatenate([r[...] for r in rows_refs], axis=0)
    blocks, biases = joined_blocks(valid_ref, frame_refs, 1)
    out_ref[...] = jnp.zeros_like(out_ref)
    for h in range(heads):
        cut = slice(h * HD, (h + 1) * HD)
        cut2 = slice(width + h * HD, width + (h + 1) * HD)
        query, dout = rows[:, cut], rows[:, cut2]
        scores = [
            mm(b[:, cut], query, NT) * LOG2 + bias for b, bias in zip(blocks, biases)
        ]
        top = functools.reduce(
            jnp.maximum, [jnp.max(s, axis=0, keepdims=True) for s in scores]
        )
        top = jnp.maximum(top, 0.1 * LOW)
        total = jnp.zeros_like(top)
        delta = jnp.zeros_like(top)
        for s, b in zip(scores, blocks):
            weight = jnp.exp2(s - top)
            dprobs = mm(b[:, cut2], dout, NT)
            total += jnp.sum(weight, axis=0, keepdims=True)
            delta += jnp.sum(weight * dprobs, axis=0, keepdims=True)
        total = jnp.maximum(total, 1.0)
        out_ref[h : h + 1, :] = top + jnp.log2(total)
        out_ref[8 + h : 9 + h, :] = delta / total


def in_own_order(x, k, own):
    if k & 2:
        x = pltpu.roll(x, 2 * own, 1)
    if k & 1:
        lane = lax.broadcasted_iota(jnp.int32, x.shape, 1)
        x = jnp.where(
            lane % (2 * own) < own, pltpu.roll(x, 3 * own, 1), pltpu.roll(x, own, 1)
        )
    return x


def grads_kernel(heads, valid_ref, *refs):
    rows_refs, frame_refs, stat_refs = refs[:4], refs[4:8], refs[8:12]
    keep_refs, send_refs, dq_refs = refs[12:14], refs[14:16], refs[16:20]
    width = heads * HD
    rows = jnp.concatenate([r[...] for r in rows_refs], axis=0)
    blocks, biases = joined_blocks(valid_ref, frame_refs, SPAN)
    part = frame_refs[0].shape[0]
    own = rows_refs[0].shape[0]
    stats = [in_own_order(stat_refs[k][...], k, own) for k in range(4)]
    tops = [s[:8] for s in stats]
    top = functools.reduce(jnp.maximum, tops)
    shares = [jnp.exp2(t - top) for t in tops]
    total = functools.reduce(jnp.add, shares)
    lse = top + jnp.log2(total)
    delta = functools.reduce(
        jnp.add, [w * s[8:] for w, s in zip(shares, stats)]
    ) / total
    dq_t, att_t = [], []
    for h in range(heads):
        cut = slice(h * HD, (h + 1) * HD)
        cut2 = slice(width + h * HD, width + (h + 1) * HD)
        query, dout = rows[:, cut], rows[:, cut2]
        dq_sum = jnp.zeros((HD, rows.shape[0]), F32)
        att_sum = jnp.zeros((HD, rows.shape[0]), F32)
        for j, (b, bias) in enumerate(zip(blocks, biases)):
            key, value = b[:, cut], b[:, cut2]
            scores = mm(key, query, NT) * LOG2 + bias
            probs = jnp.exp2(scores - lse[h : h + 1])
            dprobs = mm(value, dout, NT)
            dscores = (probs * (dprobs - delta[h : h + 1])).astype(BF)
            probs = probs.astype(BF)
            dkey = mm(dscores, query) * SCALE
            dvalue = mm(probs, dout)
            for i in range(SPAN):
                owner, at = j * SPAN + i, slice(i * part, (i + 1) * part)
                out_ref = (send_refs if owner % 2 else keep_refs)[owner // 2]
                out_ref[:, cut] = dkey[at].astype(out_ref.dtype)
                out_ref[:, cut2] = dvalue[at].astype(out_ref.dtype)
            dq_sum += mm(key, dscores, TN)
            att_sum += mm(value, probs, TN)
        dq_t.append(dq_sum * SCALE)
        att_t.append(att_sum)
    joined = jnp.concatenate(dq_t + att_t, axis=0).T
    for k in range(4):
        dq_refs[k][...] = joined[k * own : (k + 1) * own].astype(dq_refs[k].dtype)


QUAD = (0, 2, 5, 7)


def fetch(pairs, sems):
    copies = [
        pltpu.make_async_copy(source, target, sems.at[i])
        for i, (source, target) in enumerate(pairs)
    ]
    for copy in copies:
        copy.start()
    return copies


def project_kernel(
    left_ref, right_ref, frames_ref, wq_ref, wo_ref, wk_ref, wv_ref, rows_ref, kv_ref,
    left, right, frames, wq, wo, wk, wv, sems,
):
    width = wq.shape[0]
    half = width // 2
    pairs = [(left_ref, left)]
    for source, target in ((wq_ref, wq), (wo_ref, wo), (wk_ref, wk), (wv_ref, wv)):
        pairs += [
            (source.at[:half], target.at[:half]),
            (source.at[half:], target.at[half:]),
        ]
        if source is wq_ref:
            pairs.append((right_ref, right))
        if source is wo_ref:
            pairs.append((frames_ref, frames))
    copies = fetch(pairs, sems)
    for i, (x, w, out, side) in enumerate(
        ((left, wq, rows_ref, 0), (right, wo, rows_ref, 1), (frames, wk, kv_ref, 0), (frames, wv, kv_ref, 1))
    ):
        for copy in copies[3 * i : 3 * i + 3]:
            copy.wait()
        out[:, side * width : (side + 1) * width] = mm(x[...], w[...], NT).astype(BF)


def collect_kernel(keep_ref, core_ref, pair_ref, dq_ref, a_ref, b_ref, c_ref, out_ref):
    slab = keep_ref.shape[0]
    total = keep_ref[...] + core_ref[...].astype(F32) + pair_ref[...].astype(F32)
    out_ref[:slab] = total.astype(out_ref.dtype)
    total = dq_ref[...] + a_ref[...].astype(F32) + b_ref[...].astype(F32)
    out_ref[slab:] = (total + c_ref[...].astype(F32)).astype(out_ref.dtype)


def weights_kernel(part, xt_ref, xt2_ref, y_ref, y2_ref, *out_refs):
    kv_refs, keep_ref, send_ref = out_refs[:4], out_refs[4], out_refs[5]
    frames = y_ref.shape[0] - part
    half = y_ref.shape[1] // 2
    step = kv_refs[0].shape[0]
    pairs = ((xt_ref, y_ref), (xt2_ref, y2_ref))
    for k in (3, 1, 2, 0):
        span = slice(k * step, (k + 1) * step)
        kv = sum(mm(x[span, :frames], y[:frames, :]) for x, y in pairs)
        kv_refs[k][...] = kv.astype(kv_refs[k].dtype)
        q = sum(
            mm(x[span, frames : frames + part], y[frames:, :half]) for x, y in pairs
        )
        o = sum(mm(x[span, frames + part :], y[frames:, half:]) for x, y in pairs)
        near = slice(k * step // 2, (k + 1) * step // 2)
        keep_ref[near, :half] = q[: step // 2]
        keep_ref[near, half:] = o[: step // 2]
        send_ref[near, :half] = q[step // 2 :].astype(send_ref.dtype)
        send_ref[near, half:] = o[step // 2 :].astype(send_ref.dtype)


def inputs_kernel(where_ref, y_ref, wk_ref, wv_ref, wq_ref, own_ref, *refs):
    send_refs, (scratch, wk, wv, wq, sems) = refs[:3], refs[3:]
    width = wk.shape[0]
    half = width // 2
    pairs = []
    for source, target in ((wk_ref, wk), (wv_ref, wv), (wq_ref, wq)):
        pairs += [
            (source.at[:half], target.at[:half]),
            (source.at[half:], target.at[half:]),
        ]
    copies = fetch(pairs, sems)
    part = y_ref.shape[0] // 5 * 4
    dkey, dvalue = y_ref[:part, :width], y_ref[:part, width:]
    dquery = y_ref[part:, :width]
    for copy in copies:
        copy.wait()
    for t in range(4):
        span = slice(t * width, (t + 1) * width)
        scratch[t, :part] = mm(dkey, wk[:, span]) + mm(dvalue, wv[:, span])
        scratch[t, part:] = mm(dquery, wq[:, span])
    own_ref[...] = scratch[where_ref[0]]
    for k in (1, 2, 3):
        send_refs[k - 1][...] = scratch[where_ref[0] ^ k].astype(BF)


VMEM = pl.BlockSpec(memory_space=pltpu.VMEM)
SMEM = pl.BlockSpec(memory_space=pltpu.SMEM)


def per_device(query_in, grad_out, encoder_states, frame_lengths, w_query, w_key, w_value, w_out):
    rows_in, rows_grad, frames = query_in[0], grad_out[0], encoder_states[0]
    width = w_query.shape[1]
    heads = width // HD
    model = w_query.shape[0]
    inner = model // 64
    own, slab = rows_in.shape[0], frames.shape[0]
    quarter = slab // 4
    xi, zi, ci, yi = (lax.axis_index(n) for n in ("dp", "z", "core", "head"))
    wq_t, wk_t, wv_t = w_query.T, w_key.T, w_value.T
    where = yi.reshape(1).astype(jnp.int32)

    def call(kernel, outs, ins, scalar=False, scratch=(), work=2):
        shapes = [jax.ShapeDtypeStruct(shape, kind) for shape, kind in outs]
        specs = [SMEM] * scalar + [VMEM] * (len(ins) - scalar)
        return pl.pallas_call(
            kernel,
            out_shape=shapes,
            in_specs=specs,
            out_specs=[VMEM] * len(outs),
            scratch_shapes=scratch,
            compiler_params=pltpu.CompilerParams(vmem_limit_bytes=24 * 1024 * 1024),
            cost_estimate=pl.CostEstimate(
                flops=work, bytes_accessed=0, transcendentals=0
            ),
        )(*ins)

    hbm = pl.BlockSpec(memory_space=pl.ANY)
    weights = [pltpu.VMEM((width, model), BF)] * 4
    rows0, kv = pl.pallas_call(
        project_kernel,
        out_shape=[
            jax.ShapeDtypeStruct((own, 2 * width), BF),
            jax.ShapeDtypeStruct((slab, 2 * width), BF),
        ],
        in_specs=[hbm] * 7,
        out_specs=[VMEM] * 2,
        scratch_shapes=[pltpu.VMEM((rows, model), BF) for rows in (own, own, slab)]
        + weights
        + [pltpu.SemaphoreType.DMA((12,))],
        compiler_params=pltpu.CompilerParams(vmem_limit_bytes=56 * 1024 * 1024),
    )(rows_in, rows_grad, frames, wq_t, w_out, wk_t, wv_t)

    kv_pair = flip(kv, "z", 8, 1)
    kv_core = swap(kv, "core")
    rows0, kv_core = lax.optimization_barrier((rows0, kv_core))
    row_blocks = [rows0] + [flip(rows0, "z", 8, QUAD[j]) for j in (1, 2, 3)]

    def turn(stacked, c_rel):
        place = jnp.arange(model // 2, dtype=jnp.int32)
        unit, rest = place % inner, place // inner
        a_rel, b_rel = rest % 4, (rest // 4) % 2
        x_rel = rest // 8
        target = (
            (x_rel ^ xi) * 16 + ((2 * (a_rel % 2)) ^ (5 * (a_rel // 2)) ^ b_rel ^ zi) * 2 + (c_rel ^ ci)
        ) * inner + unit
        pick = (jnp.arange(model, dtype=jnp.int32)[None, :] == target[:, None]).astype(BF)
        return mm(pick, stacked, NT).astype(BF)

    stacked = jnp.concatenate([frames, rows_in, rows_grad], axis=0)
    xt, xt_send = turn(stacked, 0), turn(stacked, 1)
    row_blocks[1:], kv_pair, kv_core, xt, xt_send = lax.optimization_barrier(
        (row_blocks[1:], kv_pair, kv_core, xt, xt_send)
    )
    frame_blocks = [kv, kv_core, kv_pair, swap(kv_pair, "core")]
    starts = [
        slab * (2 * (zi ^ db) + (ci ^ dc)) for db in (0, 1) for dc in (0, 1)
    ]
    valid = jnp.stack([frame_lengths[0] - s for s in starts]).astype(jnp.int32)

    (stats,) = call(
        functools.partial(stats_kernel, heads),
        [((16, 4 * own), F32)],
        (valid, *row_blocks, *frame_blocks),
        True,
    )
    stats, xt_send = lax.optimization_barrier((stats, xt_send))
    xt_other = swap(xt_send, "core")
    all_stats = [stats] + [flip(stats, "z", 8, QUAD[j]) for j in (1, 2, 3)]

    all_stats[1:], xt_other = lax.optimization_barrier((all_stats[1:], xt_other))

    keep0, keep1, send0, send1, dq0, *dq_sends = call(
        functools.partial(grads_kernel, heads),
        [((slab, 2 * width), F32)] * 2
        + [((slab, 2 * width), BF)] * 2
        + [((own, 2 * width), F32)]
        + [((own, 2 * width), BF)] * 3,
        (valid, *row_blocks, *frame_blocks, *all_stats),
        True,
    )

    pair = (keep1 + swap(send1, "core").astype(F32)).astype(BF)
    dq_sends, send0, pair = lax.optimization_barrier((dq_sends, send0, pair))
    recv = swap(send0, "core")
    pair_recv = flip(pair, "z", 8, 1)
    dq_recv = [flip(d, "z", 8, QUAD[k]) for k, d in zip((1, 2, 3), dq_sends)]
    (grads,) = call(
        collect_kernel,
        [((slab + own, 2 * width), BF)],
        (keep0, recv, pair_recv, dq0, *dq_recv),
    )
    grads_other = swap(grads, "core")

    part = model // 8
    kv_own, *kv_sends, qo_keep, qo_send = call(
        functools.partial(weights_kernel, own),
        [((part, 2 * width), F32)]
        + [((part, 2 * width), BF)] * 3
        + [((2 * part, 2 * width), F32), ((2 * part, 2 * width), BF)],
        (xt, xt_other, grads, grads_other),
    )
    kv_x = [flip(kv_sends[k - 1], "dp", 4, k) for k in (2, 1, 3)]
    qo_b = flip(qo_send, "z", 8, 1)

    held, kv_own = lax.optimization_barrier((grads, kv_own))
    own_part, *sends = pl.pallas_call(
        inputs_kernel,
        out_shape=[jax.ShapeDtypeStruct((slab + own, width), F32)]
        + [jax.ShapeDtypeStruct((slab + own, width), BF)] * 3,
        in_specs=[SMEM, VMEM] + [pl.BlockSpec(memory_space=pltpu.HBM)] * 3,
        out_specs=[VMEM] * 4,
        scratch_shapes=[pltpu.VMEM((4, slab + own, width), F32)]
        + weights[:3]
        + [pltpu.SemaphoreType.DMA((6,))],
        compiler_params=pltpu.CompilerParams(vmem_limit_bytes=24 * 1024 * 1024),
        cost_estimate=pl.CostEstimate(
            flops=12_000_000_000, bytes_accessed=0, transcendentals=0
        ),
    )(where, held, wk_t, wv_t, wq_t)
    arrived = [flip(sends[k - 1], "head", 4, k) for k in (2, 1)]

    cut = part // 2
    kv_sum = kv_own + sum(k.astype(F32) for k in kv_x)
    kv_b = flip(kv_sum[cut:].astype(BF), "z", 8, 1)
    qo_sum = qo_keep + qo_b.astype(F32)
    qo_x = [flip(qo_sum[k * cut : (k + 1) * cut].astype(BF), "dp", 4, k) for k in (2, 1, 3)]
    kv_sum = kv_sum[:cut] + kv_b.astype(F32)
    qo_sum = qo_sum[:cut] + sum(q.astype(F32) for q in qo_x)
    total = jnp.concatenate([kv_sum, qo_sum], axis=1)
    total, sends[2], arrived = lax.optimization_barrier((total, sends[2], arrived))
    arrived.append(flip(sends[2], "head", 4, 3))
    low = total.astype(BF)
    over = [flip(low[k * inner : (k + 1) * inner], "z", 8, QUAD[k]) for k in (2, 1, 3)]
    total = total[:inner] + sum(p.astype(F32) for p in over)
    dframes = (own_part[:slab] + sum(p[:slab].astype(F32) for p in arrived)).astype(BF)
    dinput = (own_part[slab:] + sum(p[slab:].astype(F32) for p in arrived)).astype(BF)
    return (
        dinput[None],
        dframes[None],
        total[:, 2 * width : 3 * width],
        total[:, :width],
        total[:, width : 2 * width],
        total[:, 3 * width :].T,
    )


def solution(mesh):
    dp, tm, head = mesh.devices.shape
    fine = Mesh(mesh.devices.reshape(dp, tm // 2, 2, head), ("dp", "z", "core", "head"))
    tm = ("z", "core")
    placed = (
        P("dp", tm, None),
        P("dp", tm, None),
        P("dp", tm, None),
        P("dp"),
        P(None, "head"),
        P(None, "head"),
        P(None, "head"),
        P("head", None),
    )
    every = ("dp",) + tm
    return jax.shard_map(
        per_device,
        mesh=fine,
        in_specs=placed,
        out_specs=(
            P("dp", tm, "head"),
            P("dp", tm, "head"),
            P(every, "head"),
            P(every, "head"),
            P(every, "head"),
            P("head", every),
        ),
        check_vma=False,
    )
```

```python
import functools
import math

import jax
import jax.numpy as jnp
from jax import lax
from jax.experimental import pallas as pl
from jax.experimental.pallas import tpu as pltpu
from jax.sharding import Mesh, PartitionSpec as P

HD = 64
BF = jnp.bfloat16
F32 = jnp.float32
SCALE = HD ** (-0.5)
LOG2 = SCALE * math.log2(math.e)
LOW = -1e30
NT = (((1,), (1,)), ((), ()))
TN = (((0,), (0,)), ((), ()))


def mm(left, right, dims=None):
    if dims is None:
        dims = (((1,), (0,)), ((), ()))
    return lax.dot_general(left, right, dims, preferred_element_type=F32)


def flip(x, axis, size, bits):
    return lax.ppermute(x, axis, [(i, i ^ bits) for i in range(size)])


def swap(x, axis):
    return flip(x, axis, 2, 1)


def frame_bias(valid_ref, block, rows):
    positions = lax.broadcasted_iota(jnp.int32, (rows, 1), 0)
    return jnp.where(positions < valid_ref[block], 0.0, LOW)


SPAN = 2


def joined_blocks(valid_ref, refs, span):
    blocks, biases = [], []
    for first in range(0, len(refs), span):
        some = range(first, first + span)
        blocks.append(jnp.concatenate([refs[j][...] for j in some], axis=0))
        biases.append(
            jnp.concatenate([frame_bias(valid_ref, j, refs[j].shape[0]) for j in some], axis=0)
        )
    return blocks, biases


def stats_kernel(heads, valid_ref, *refs):
    rows_refs, frame_refs, out_ref = refs[:4], refs[4:8], refs[8]
    width = heads * HD
    rows = jnp.concatenate([r[...] for r in rows_refs], axis=0)
    blocks, biases = joined_blocks(valid_ref, frame_refs, 1)
    out_ref[...] = jnp.zeros_like(out_ref)
    for h in range(heads):
        cut = slice(h * HD, (h + 1) * HD)
        cut2 = slice(width + h * HD, width + (h + 1) * HD)
        query, dout = rows[:, cut], rows[:, cut2]
        scores = [
            mm(b[:, cut], query, NT) * LOG2 + bias for b, bias in zip(blocks, biases)
        ]
        top = functools.reduce(
            jnp.maximum, [jnp.max(s, axis=0, keepdims=True) for s in scores]
        )
        top = jnp.maximum(top, 0.1 * LOW)
        total = jnp.zeros_like(top)
        delta = jnp.zeros_like(top)
        for s, b in zip(scores, blocks):
            weight = jnp.exp2(s - top)
            dprobs = mm(b[:, cut2], dout, NT)
            total += jnp.sum(weight, axis=0, keepdims=True)
            delta += jnp.sum(weight * dprobs, axis=0, keepdims=True)
        total = jnp.maximum(total, 1.0)
        out_ref[h : h + 1, :] = top + jnp.log2(total)
        out_ref[8 + h : 9 + h, :] = delta / total


def in_own_order(x, k, own):
    if k & 2:
        x = pltpu.roll(x, 2 * own, 1)
    if k & 1:
        lane = lax.broadcasted_iota(jnp.int32, x.shape, 1)
        x = jnp.where(
            lane % (2 * own) < own, pltpu.roll(x, 3 * own, 1), pltpu.roll(x, own, 1)
        )
    return x


def grads_kernel(heads, valid_ref, *refs):
    rows_refs, frame_refs, stat_refs = refs[:4], refs[4:8], refs[8:12]
    keep_refs, send_refs, dq_refs = refs[12:14], refs[14:16], refs[16:20]
    width = heads * HD
    rows = jnp.concatenate([r[...] for r in rows_refs], axis=0)
    blocks, biases = joined_blocks(valid_ref, frame_refs, SPAN)
    part = frame_refs[0].shape[0]
    own = rows_refs[0].shape[0]
    stats = [in_own_order(stat_refs[k][...], k, own) for k in range(4)]
    tops = [s[:8] for s in stats]
    top = functools.reduce(jnp.maximum, tops)
    shares = [jnp.exp2(t - top) for t in tops]
    total = functools.reduce(jnp.add, shares)
    lse = top + jnp.log2(total)
    delta = functools.reduce(
        jnp.add, [w * s[8:] for w, s in zip(shares, stats)]
    ) / total
    dq_t, att_t = [], []
    for h in range(heads):
        cut = slice(h * HD, (h + 1) * HD)
        cut2 = slice(width + h * HD, width + (h + 1) * HD)
        query, dout = rows[:, cut], rows[:, cut2]
        dq_sum = jnp.zeros((HD, rows.shape[0]), F32)
        att_sum = jnp.zeros((HD, rows.shape[0]), F32)
        for j, (b, bias) in enumerate(zip(blocks, biases)):
            key, value = b[:, cut], b[:, cut2]
            scores = mm(key, query, NT) * LOG2 + bias
            probs = jnp.exp2(scores - lse[h : h + 1])
            dprobs = mm(value, dout, NT)
            dscores = (probs * (dprobs - delta[h : h + 1])).astype(BF)
            probs = probs.astype(BF)
            dkey = mm(dscores, query) * SCALE
            dvalue = mm(probs, dout)
            for i in range(SPAN):
                owner, at = j * SPAN + i, slice(i * part, (i + 1) * part)
                out_ref = (send_refs if owner % 2 else keep_refs)[owner // 2]
                out_ref[:, cut] = dkey[at].astype(out_ref.dtype)
                out_ref[:, cut2] = dvalue[at].astype(out_ref.dtype)
            dq_sum += mm(key, dscores, TN)
            att_sum += mm(value, probs, TN)
        dq_t.append(dq_sum * SCALE)
        att_t.append(att_sum)
    joined = jnp.concatenate(dq_t + att_t, axis=0).T
    for k in range(4):
        dq_refs[k][...] = joined[k * own : (k + 1) * own].astype(dq_refs[k].dtype)


QUAD = (0, 2, 5, 7)


def fetch(pairs, sems):
    copies = [
        pltpu.make_async_copy(source, target, sems.at[i])
        for i, (source, target) in enumerate(pairs)
    ]
    for copy in copies:
        copy.start()
    return copies


def project_kernel(
    left_ref, right_ref, frames_ref, wq_ref, wo_ref, wk_ref, wv_ref, rows_ref, kv_ref,
    left, right, frames, wq, wo, wk, wv, sems,
):
    width = wq.shape[0]
    step = width // 4
    groups = []
    for x, w in (
        ((left_ref, left), (wq_ref, wq)),
        ((right_ref, right), (wo_ref, wo)),
        ((frames_ref, frames), (wk_ref, wk)),
        (None, (wv_ref, wv)),
    ):
        group = [x] if x else []
        for i in range(4):
            part = slice(i * step, (i + 1) * step)
            group.append((w[0].at[part], w[1].at[part]))
        groups.append(group)
    copies = fetch([pair for group in groups for pair in group], sems)
    first = 0
    for group, (x, w, out, side) in zip(
        groups,
        ((left, wq, rows_ref, 0), (right, wo, rows_ref, 1), (frames, wk, kv_ref, 0), (frames, wv, kv_ref, 1)),
    ):
        for copy in copies[first : first + len(group)]:
            copy.wait()
        first += len(group)
        out[:, side * width : (side + 1) * width] = mm(x[...], w[...], NT).astype(BF)


def collect_kernel(keep_ref, core_ref, pair_ref, dq_ref, a_ref, b_ref, c_ref, out_ref):
    slab = keep_ref.shape[0]
    total = keep_ref[...] + core_ref[...].astype(F32) + pair_ref[...].astype(F32)
    out_ref[:slab] = total.astype(out_ref.dtype)
    total = dq_ref[...] + a_ref[...].astype(F32) + b_ref[...].astype(F32)
    out_ref[slab:] = (total + c_ref[...].astype(F32)).astype(out_ref.dtype)


def weights_kernel(part, xt_ref, xt2_ref, y_ref, y2_ref, *out_refs):
    kv_refs, keep_ref, send_ref = out_refs[:4], out_refs[4], out_refs[5]
    frames = y_ref.shape[0] - part
    half = y_ref.shape[1] // 2
    step = kv_refs[0].shape[0]
    pairs = ((xt_ref, y_ref), (xt2_ref, y2_ref))
    for k in (3, 1, 2, 0):
        span = slice(k * step, (k + 1) * step)
        kv = sum(mm(x[span, :frames], y[:frames, :]) for x, y in pairs)
        kv_refs[k][...] = kv.astype(kv_refs[k].dtype)
        q = sum(
            mm(x[span, frames : frames + part], y[frames:, :half]) for x, y in pairs
        )
        o = sum(mm(x[span, frames + part :], y[frames:, half:]) for x, y in pairs)
        near = slice(k * step // 2, (k + 1) * step // 2)
        keep_ref[near, :half] = q[: step // 2]
        keep_ref[near, half:] = o[: step // 2]
        send_ref[near, :half] = q[step // 2 :].astype(send_ref.dtype)
        send_ref[near, half:] = o[step // 2 :].astype(send_ref.dtype)


def inputs_kernel(where_ref, y_ref, wk_ref, wv_ref, wq_ref, own_ref, *refs):
    send_refs, (scratch, wk, wv, wq, sems) = refs[:3], refs[3:]
    width = wk.shape[0]
    half = width // 2
    pairs = []
    for source, target in ((wk_ref, wk), (wv_ref, wv), (wq_ref, wq)):
        pairs += [
            (source.at[:half], target.at[:half]),
            (source.at[half:], target.at[half:]),
        ]
    copies = fetch(pairs, sems)
    part = y_ref.shape[0] // 5 * 4
    dkey, dvalue = y_ref[:part, :width], y_ref[:part, width:]
    dquery = y_ref[part:, :width]
    for copy in copies:
        copy.wait()
    for t in range(4):
        span = slice(t * width, (t + 1) * width)
        scratch[t, :part] = mm(dkey, wk[:, span]) + mm(dvalue, wv[:, span])
        scratch[t, part:] = mm(dquery, wq[:, span])
    own_ref[...] = scratch[where_ref[0]]
    for k in (1, 2, 3):
        send_refs[k - 1][...] = scratch[where_ref[0] ^ k].astype(BF)


VMEM = pl.BlockSpec(memory_space=pltpu.VMEM)
SMEM = pl.BlockSpec(memory_space=pltpu.SMEM)


def per_device(query_in, grad_out, encoder_states, frame_lengths, w_query, w_key, w_value, w_out):
    rows_in, rows_grad, frames = query_in[0], grad_out[0], encoder_states[0]
    width = w_query.shape[1]
    heads = width // HD
    model = w_query.shape[0]
    inner = model // 64
    own, slab = rows_in.shape[0], frames.shape[0]
    quarter = slab // 4
    xi, zi, ci, yi = (lax.axis_index(n) for n in ("dp", "z", "core", "head"))
    wq_t, wk_t, wv_t = w_query.T, w_key.T, w_value.T
    where = yi.reshape(1).astype(jnp.int32)

    def call(kernel, outs, ins, scalar=False, scratch=(), work=2):
        shapes = [jax.ShapeDtypeStruct(shape, kind) for shape, kind in outs]
        specs = [SMEM] * scalar + [VMEM] * (len(ins) - scalar)
        return pl.pallas_call(
            kernel,
            out_shape=shapes,
            in_specs=specs,
            out_specs=[VMEM] * len(outs),
            scratch_shapes=scratch,
            compiler_params=pltpu.CompilerParams(vmem_limit_bytes=24 * 1024 * 1024),
            cost_estimate=pl.CostEstimate(
                flops=work, bytes_accessed=0, transcendentals=0
            ),
        )(*ins)

    hbm = pl.BlockSpec(memory_space=pl.ANY)
    weights = [pltpu.VMEM((width, model), BF)] * 4
    rows0, kv = pl.pallas_call(
        project_kernel,
        out_shape=[
            jax.ShapeDtypeStruct((own, 2 * width), BF),
            jax.ShapeDtypeStruct((slab, 2 * width), BF),
        ],
        in_specs=[hbm] * 7,
        out_specs=[VMEM] * 2,
        scratch_shapes=[pltpu.VMEM((rows, model), BF) for rows in (own, own, slab)]
        + weights
        + [pltpu.SemaphoreType.DMA((19,))],
        compiler_params=pltpu.CompilerParams(vmem_limit_bytes=56 * 1024 * 1024),
    )(rows_in, rows_grad, frames, wq_t, w_out, wk_t, wv_t)

    kv_pair = flip(kv, "z", 8, 1)
    kv_core = swap(kv, "core")
    rows0, kv_core = lax.optimization_barrier((rows0, kv_core))
    row_blocks = [rows0] + [flip(rows0, "z", 8, QUAD[j]) for j in (1, 2, 3)]

    def turn(stacked, c_rel):
        place = jnp.arange(model // 2, dtype=jnp.int32)
        unit, rest = place % inner, place // inner
        a_rel, b_rel = rest % 4, (rest // 4) % 2
        x_rel = rest // 8
        target = (
            (x_rel ^ xi) * 16 + ((2 * (a_rel % 2)) ^ (5 * (a_rel // 2)) ^ b_rel ^ zi) * 2 + (c_rel ^ ci)
        ) * inner + unit
        pick = (jnp.arange(model, dtype=jnp.int32)[None, :] == target[:, None]).astype(BF)
        return mm(pick, stacked, NT).astype(BF)

    stacked = jnp.concatenate([frames, rows_in, rows_grad], axis=0)
    xt, xt_send = turn(stacked, 0), turn(stacked, 1)
    row_blocks[1:], kv_pair, kv_core, xt, xt_send = lax.optimization_barrier(
        (row_blocks[1:], kv_pair, kv_core, xt, xt_send)
    )
    frame_blocks = [kv, kv_core, kv_pair, swap(kv_pair, "core")]
    starts = [
        slab * (2 * (zi ^ db) + (ci ^ dc)) for db in (0, 1) for dc in (0, 1)
    ]
    valid = jnp.stack([frame_lengths[0] - s for s in starts]).astype(jnp.int32)

    (stats,) = call(
        functools.partial(stats_kernel, heads),
        [((16, 4 * own), F32)],
        (valid, *row_blocks, *frame_blocks),
        True,
    )
    stats, xt_send = lax.optimization_barrier((stats, xt_send))
    xt_other = swap(xt_send, "core")
    all_stats = [stats] + [flip(stats, "z", 8, QUAD[j]) for j in (1, 2, 3)]

    all_stats[1:], xt_other = lax.optimization_barrier((all_stats[1:], xt_other))

    keep0, keep1, send0, send1, dq0, *dq_sends = call(
        functools.partial(grads_kernel, heads),
        [((slab, 2 * width), F32)] * 2
        + [((slab, 2 * width), BF)] * 2
        + [((own, 2 * width), F32)]
        + [((own, 2 * width), BF)] * 3,
        (valid, *row_blocks, *frame_blocks, *all_stats),
        True,
    )

    pair = (keep1 + swap(send1, "core").astype(F32)).astype(BF)
    dq_sends, send0, pair = lax.optimization_barrier((dq_sends, send0, pair))
    recv = swap(send0, "core")
    pair_recv = flip(pair, "z", 8, 1)
    dq_recv = [flip(d, "z", 8, QUAD[k]) for k, d in zip((1, 2, 3), dq_sends)]
    (grads,) = call(
        collect_kernel,
        [((slab + own, 2 * width), BF)],
        (keep0, recv, pair_recv, dq0, *dq_recv),
    )
    grads_other = swap(grads, "core")

    part = model // 8
    kv_own, *kv_sends, qo_keep, qo_send = call(
        functools.partial(weights_kernel, own),
        [((part, 2 * width), F32)]
        + [((part, 2 * width), BF)] * 3
        + [((2 * part, 2 * width), F32), ((2 * part, 2 * width), BF)],
        (xt, xt_other, grads, grads_other),
    )
    kv_x = [flip(kv_sends[k - 1], "dp", 4, k) for k in (2, 1, 3)]
    qo_b = flip(qo_send, "z", 8, 1)

    held, kv_own = lax.optimization_barrier((grads, kv_own))
    own_part, *sends = pl.pallas_call(
        inputs_kernel,
        out_shape=[jax.ShapeDtypeStruct((slab + own, width), F32)]
        + [jax.ShapeDtypeStruct((slab + own, width), BF)] * 3,
        in_specs=[SMEM, VMEM] + [pl.BlockSpec(memory_space=pltpu.HBM)] * 3,
        out_specs=[VMEM] * 4,
        scratch_shapes=[pltpu.VMEM((4, slab + own, width), F32)]
        + weights[:3]
        + [pltpu.SemaphoreType.DMA((6,))],
        compiler_params=pltpu.CompilerParams(vmem_limit_bytes=24 * 1024 * 1024),
        cost_estimate=pl.CostEstimate(
            flops=12_000_000_000, bytes_accessed=0, transcendentals=0
        ),
    )(where, held, wk_t, wv_t, wq_t)
    arrived = [flip(sends[k - 1], "head", 4, k) for k in (2, 1)]

    cut = part // 2
    kv_sum = kv_own + sum(k.astype(F32) for k in kv_x)
    kv_b = flip(kv_sum[cut:].astype(BF), "z", 8, 1)
    qo_sum = qo_keep + qo_b.astype(F32)
    qo_x = [flip(qo_sum[k * cut : (k + 1) * cut].astype(BF), "dp", 4, k) for k in (2, 1, 3)]
    kv_sum = kv_sum[:cut] + kv_b.astype(F32)
    qo_sum = qo_sum[:cut] + sum(q.astype(F32) for q in qo_x)
    total = jnp.concatenate([kv_sum, qo_sum], axis=1)
    total, sends[2], arrived = lax.optimization_barrier((total, sends[2], arrived))
    arrived.append(flip(sends[2], "head", 4, 3))
    low = total.astype(BF)
    over = [flip(low[k * inner : (k + 1) * inner], "z", 8, QUAD[k]) for k in (2, 1, 3)]
    total = total[:inner] + sum(p.astype(F32) for p in over)
    dframes = (own_part[:slab] + sum(p[:slab].astype(F32) for p in arrived)).astype(BF)
    dinput = (own_part[slab:] + sum(p[slab:].astype(F32) for p in arrived)).astype(BF)
    return (
        dinput[None],
        dframes[None],
        total[:, 2 * width : 3 * width],
        total[:, :width],
        total[:, width : 2 * width],
        total[:, 3 * width :].T,
    )


def solution(mesh):
    dp, tm, head = mesh.devices.shape
    fine = Mesh(mesh.devices.reshape(dp, tm // 2, 2, head), ("dp", "z", "core", "head"))
    tm = ("z", "core")
    placed = (
        P("dp", tm, None),
        P("dp", tm, None),
        P("dp", tm, None),
        P("dp"),
        P(None, "head"),
        P(None, "head"),
        P(None, "head"),
        P("head", None),
    )
    every = ("dp",) + tm
    return jax.shard_map(
        per_device,
        mesh=fine,
        in_specs=placed,
        out_specs=(
            P("dp", tm, "head"),
            P("dp", tm, "head"),
            P(every, "head"),
            P(every, "head"),
            P(every, "head"),
            P("head", every),
        ),
        check_vma=False,
    )
```

```python
import functools
import math

import jax
import jax.numpy as jnp
from jax import lax
from jax.experimental import pallas as pl
from jax.experimental.pallas import tpu as pltpu
from jax.sharding import Mesh, PartitionSpec as P

HD = 64
BF = jnp.bfloat16
F32 = jnp.float32
SCALE = HD ** (-0.5)
LOG2 = SCALE * math.log2(math.e)
LOW = -1e30
NT = (((1,), (1,)), ((), ()))
TN = (((0,), (0,)), ((), ()))


def mm(left, right, dims=None):
    if dims is None:
        dims = (((1,), (0,)), ((), ()))
    return lax.dot_general(left, right, dims, preferred_element_type=F32)


def flip(x, axis, size, bits):
    return lax.ppermute(x, axis, [(i, i ^ bits) for i in range(size)])


def swap(x, axis):
    return flip(x, axis, 2, 1)


def frame_bias(valid_ref, block, rows):
    positions = lax.broadcasted_iota(jnp.int32, (rows, 1), 0)
    return jnp.where(positions < valid_ref[block], 0.0, LOW)


SPAN = 2


def joined_blocks(valid_ref, refs, span):
    blocks, biases = [], []
    for first in range(0, len(refs), span):
        some = range(first, first + span)
        blocks.append(jnp.concatenate([refs[j][...] for j in some], axis=0))
        biases.append(
            jnp.concatenate([frame_bias(valid_ref, j, refs[j].shape[0]) for j in some], axis=0)
        )
    return blocks, biases


def stats_kernel(heads, valid_ref, *refs):
    rows_refs, frame_refs, out_ref = refs[:4], refs[4:8], refs[8]
    width = heads * HD
    rows = jnp.concatenate([r[...] for r in rows_refs], axis=0)
    blocks, biases = joined_blocks(valid_ref, frame_refs, 1)
    out_ref[...] = jnp.zeros_like(out_ref)
    for h in range(heads):
        cut = slice(h * HD, (h + 1) * HD)
        cut2 = slice(width + h * HD, width + (h + 1) * HD)
        query, dout = rows[:, cut], rows[:, cut2]
        scores = [
            mm(b[:, cut], query, NT) * LOG2 + bias for b, bias in zip(blocks, biases)
        ]
        top = functools.reduce(
            jnp.maximum, [jnp.max(s, axis=0, keepdims=True) for s in scores]
        )
        top = jnp.maximum(top, 0.1 * LOW)
        total = jnp.zeros_like(top)
        delta = jnp.zeros_like(top)
        for s, b in zip(scores, blocks):
            weight = jnp.exp2(s - top)
            dprobs = mm(b[:, cut2], dout, NT)
            total += jnp.sum(weight, axis=0, keepdims=True)
            delta += jnp.sum(weight * dprobs, axis=0, keepdims=True)
        total = jnp.maximum(total, 1.0)
        out_ref[h : h + 1, :] = top + jnp.log2(total)
        out_ref[8 + h : 9 + h, :] = delta / total


def in_own_order(x, k, own):
    if k & 2:
        x = pltpu.roll(x, 2 * own, 1)
    if k & 1:
        lane = lax.broadcasted_iota(jnp.int32, x.shape, 1)
        x = jnp.where(
            lane % (2 * own) < own, pltpu.roll(x, 3 * own, 1), pltpu.roll(x, own, 1)
        )
    return x


def grads_kernel(heads, valid_ref, *refs):
    rows_refs, frame_refs, stat_refs = refs[:4], refs[4:8], refs[8:12]
    keep_refs, send_refs, dq_refs = refs[12:14], refs[14:16], refs[16:20]
    width = heads * HD
    rows = jnp.concatenate([r[...] for r in rows_refs], axis=0)
    blocks, biases = joined_blocks(valid_ref, frame_refs, SPAN)
    part = frame_refs[0].shape[0]
    own = rows_refs[0].shape[0]
    stats = [in_own_order(stat_refs[k][...], k, own) for k in range(4)]
    tops = [s[:8] for s in stats]
    top = functools.reduce(jnp.maximum, tops)
    shares = [jnp.exp2(t - top) for t in tops]
    total = functools.reduce(jnp.add, shares)
    lse = top + jnp.log2(total)
    delta = functools.reduce(
        jnp.add, [w * s[8:] for w, s in zip(shares, stats)]
    ) / total
    dq_t, att_t = [], []
    for h in range(heads):
        cut = slice(h * HD, (h + 1) * HD)
        cut2 = slice(width + h * HD, width + (h + 1) * HD)
        query, dout = rows[:, cut], rows[:, cut2]
        dq_sum = jnp.zeros((HD, rows.shape[0]), F32)
        att_sum = jnp.zeros((HD, rows.shape[0]), F32)
        for j, (b, bias) in enumerate(zip(blocks, biases)):
            key, value = b[:, cut], b[:, cut2]
            scores = mm(key, query, NT) * LOG2 + bias
            probs = jnp.exp2(scores - lse[h : h + 1])
            dprobs = mm(value, dout, NT)
            dscores = (probs * (dprobs - delta[h : h + 1])).astype(BF)
            probs = probs.astype(BF)
            dkey = mm(dscores, query) * SCALE
            dvalue = mm(probs, dout)
            for i in range(SPAN):
                owner, at = j * SPAN + i, slice(i * part, (i + 1) * part)
                out_ref = (send_refs if owner % 2 else keep_refs)[owner // 2]
                out_ref[:, cut] = dkey[at].astype(out_ref.dtype)
                out_ref[:, cut2] = dvalue[at].astype(out_ref.dtype)
            dq_sum += mm(key, dscores, TN)
            att_sum += mm(value, probs, TN)
        dq_t.append(dq_sum * SCALE)
        att_t.append(att_sum)
    joined = jnp.concatenate(dq_t + att_t, axis=0).T
    for k in range(4):
        dq_refs[k][...] = joined[k * own : (k + 1) * own].astype(dq_refs[k].dtype)


QUAD = (0, 2, 5, 7)


def fetch(pairs, sems):
    copies = [
        pltpu.make_async_copy(source, target, sems.at[i])
        for i, (source, target) in enumerate(pairs)
    ]
    for copy in copies:
        copy.start()
    return copies


def project_kernel(
    left_ref, right_ref, frames_ref, wq_ref, wo_ref, wk_ref, wv_ref, rows_ref, kv_ref,
    left, right, frames, wq, wo, wk, wv, sems,
):
    width = wq.shape[0]
    step = width // 4
    groups = []
    for x, w in (
        ((left_ref, left), (wq_ref, wq)),
        ((right_ref, right), (wo_ref, wo)),
        ((frames_ref, frames), (wk_ref, wk)),
        (None, (wv_ref, wv)),
    ):
        group = [x] if x else []
        for i in range(4):
            part = slice(i * step, (i + 1) * step)
            group.append((w[0].at[part], w[1].at[part]))
        groups.append(group)
    copies = fetch([pair for group in groups for pair in group], sems)
    first = 0
    for group, (x, w, out, side) in zip(
        groups,
        ((left, wq, rows_ref, 0), (right, wo, rows_ref, 1), (frames, wk, kv_ref, 0), (frames, wv, kv_ref, 1)),
    ):
        for copy in copies[first : first + len(group)]:
            copy.wait()
        first += len(group)
        out[:, side * width : (side + 1) * width] = mm(x[...], w[...], NT).astype(BF)


def collect_kernel(keep_ref, core_ref, pair_ref, dq_ref, a_ref, b_ref, c_ref, out_ref):
    slab = keep_ref.shape[0]
    total = keep_ref[...] + core_ref[...].astype(F32) + pair_ref[...].astype(F32)
    out_ref[:slab] = total.astype(out_ref.dtype)
    total = dq_ref[...] + a_ref[...].astype(F32) + b_ref[...].astype(F32)
    out_ref[slab:] = (total + c_ref[...].astype(F32)).astype(out_ref.dtype)


def weights_kernel(part, xt_ref, xt2_ref, y_ref, y2_ref, *out_refs):
    kv_refs, keep_ref, send_ref = out_refs[:4], out_refs[4], out_refs[5]
    frames = y_ref.shape[0] - part
    half = y_ref.shape[1] // 2
    step = kv_refs[0].shape[0]
    pairs = ((xt_ref, y_ref), (xt2_ref, y2_ref))
    for k in (3, 1, 2, 0):
        span = slice(k * step, (k + 1) * step)
        kv = sum(mm(x[span, :frames], y[:frames, :]) for x, y in pairs)
        kv_refs[k][...] = kv.astype(kv_refs[k].dtype)
        q = sum(
            mm(x[span, frames : frames + part], y[frames:, :half]) for x, y in pairs
        )
        o = sum(mm(x[span, frames + part :], y[frames:, half:]) for x, y in pairs)
        near = slice(k * step // 2, (k + 1) * step // 2)
        keep_ref[near, :half] = q[: step // 2]
        keep_ref[near, half:] = o[: step // 2]
        send_ref[near, :half] = q[step // 2 :].astype(send_ref.dtype)
        send_ref[near, half:] = o[step // 2 :].astype(send_ref.dtype)


def inputs_kernel(where_ref, y_ref, wk_ref, wv_ref, wq_ref, own_ref, *refs):
    send_refs, (scratch, wk, wv, wq, sems) = refs[:3], refs[3:]
    width = wk.shape[0]
    half = width // 2
    pairs = []
    for source, target in ((wk_ref, wk), (wv_ref, wv), (wq_ref, wq)):
        pairs += [
            (source.at[:half], target.at[:half]),
            (source.at[half:], target.at[half:]),
        ]
    copies = fetch(pairs, sems)
    part = y_ref.shape[0] // 5 * 4
    dkey, dvalue = y_ref[:part, :width], y_ref[:part, width:]
    dquery = y_ref[part:, :width]
    for copy in copies:
        copy.wait()
    for t in range(4):
        span = slice(t * width, (t + 1) * width)
        scratch[t, :part] = mm(dkey, wk[:, span]) + mm(dvalue, wv[:, span])
        scratch[t, part:] = mm(dquery, wq[:, span])
    own_ref[...] = scratch[where_ref[0]]
    for k in (1, 2, 3):
        send_refs[k - 1][...] = scratch[where_ref[0] ^ k].astype(BF)


VMEM = pl.BlockSpec(memory_space=pltpu.VMEM)
SMEM = pl.BlockSpec(memory_space=pltpu.SMEM)


def per_device(query_in, grad_out, encoder_states, frame_lengths, w_query, w_key, w_value, w_out):
    rows_in, rows_grad, frames = query_in[0], grad_out[0], encoder_states[0]
    width = w_query.shape[1]
    heads = width // HD
    model = w_query.shape[0]
    inner = model // 64
    own, slab = rows_in.shape[0], frames.shape[0]
    quarter = slab // 4
    xi, zi, ci, yi = (lax.axis_index(n) for n in ("dp", "z", "core", "head"))
    wq_t, wk_t, wv_t = w_query.T, w_key.T, w_value.T
    where = yi.reshape(1).astype(jnp.int32)

    def call(kernel, outs, ins, scalar=False, scratch=(), work=2):
        shapes = [jax.ShapeDtypeStruct(shape, kind) for shape, kind in outs]
        specs = [SMEM] * scalar + [VMEM] * (len(ins) - scalar)
        return pl.pallas_call(
            kernel,
            out_shape=shapes,
            in_specs=specs,
            out_specs=[VMEM] * len(outs),
            scratch_shapes=scratch,
            compiler_params=pltpu.CompilerParams(vmem_limit_bytes=18 * 1024 * 1024),
            cost_estimate=pl.CostEstimate(
                flops=work, bytes_accessed=0, transcendentals=0
            ),
        )(*ins)

    hbm = pl.BlockSpec(memory_space=pl.ANY)
    weights = [pltpu.VMEM((width, model), BF)] * 4
    rows0, kv = pl.pallas_call(
        project_kernel,
        out_shape=[
            jax.ShapeDtypeStruct((own, 2 * width), BF),
            jax.ShapeDtypeStruct((slab, 2 * width), BF),
        ],
        in_specs=[hbm] * 7,
        out_specs=[VMEM] * 2,
        scratch_shapes=[pltpu.VMEM((rows, model), BF) for rows in (own, own, slab)]
        + weights
        + [pltpu.SemaphoreType.DMA((19,))],
        compiler_params=pltpu.CompilerParams(vmem_limit_bytes=56 * 1024 * 1024),
    )(rows_in, rows_grad, frames, wq_t, w_out, wk_t, wv_t)

    kv_pair = flip(kv, "z", 8, 1)
    kv_core = swap(kv, "core")
    rows0, kv_core = lax.optimization_barrier((rows0, kv_core))
    row_blocks = [rows0] + [flip(rows0, "z", 8, QUAD[j]) for j in (1, 2, 3)]

    def turn(stacked, c_rel):
        place = jnp.arange(model // 2, dtype=jnp.int32)
        unit, rest = place % inner, place // inner
        a_rel, b_rel = rest % 4, (rest // 4) % 2
        x_rel = rest // 8
        target = (
            (x_rel ^ xi) * 16 + ((2 * (a_rel % 2)) ^ (5 * (a_rel // 2)) ^ b_rel ^ zi) * 2 + (c_rel ^ ci)
        ) * inner + unit
        pick = (jnp.arange(model, dtype=jnp.int32)[None, :] == target[:, None]).astype(BF)
        return mm(pick, stacked, NT).astype(BF)

    stacked = jnp.concatenate([frames, rows_in, rows_grad], axis=0)
    xt, xt_send = turn(stacked, 0), turn(stacked, 1)
    row_blocks[1:], kv_pair, kv_core, xt, xt_send = lax.optimization_barrier(
        (row_blocks[1:], kv_pair, kv_core, xt, xt_send)
    )
    frame_blocks = [kv, kv_core, kv_pair, swap(kv_pair, "core")]
    starts = [
        slab * (2 * (zi ^ db) + (ci ^ dc)) for db in (0, 1) for dc in (0, 1)
    ]
    valid = jnp.stack([frame_lengths[0] - s for s in starts]).astype(jnp.int32)

    (stats,) = call(
        functools.partial(stats_kernel, heads),
        [((16, 4 * own), F32)],
        (valid, *row_blocks, *frame_blocks),
        True,
    )
    stats, xt_send = lax.optimization_barrier((stats, xt_send))
    xt_other = swap(xt_send, "core")
    all_stats = [stats] + [flip(stats, "z", 8, QUAD[j]) for j in (1, 2, 3)]

    all_stats[1:], xt_other = lax.optimization_barrier((all_stats[1:], xt_other))

    keep0, keep1, send0, send1, dq0, *dq_sends = call(
        functools.partial(grads_kernel, heads),
        [((slab, 2 * width), F32)] * 2
        + [((slab, 2 * width), BF)] * 2
        + [((own, 2 * width), F32)]
        + [((own, 2 * width), BF)] * 3,
        (valid, *row_blocks, *frame_blocks, *all_stats),
        True,
    )

    pair = (keep1 + swap(send1, "core").astype(F32)).astype(BF)
    dq_sends, send0, pair = lax.optimization_barrier((dq_sends, send0, pair))
    recv = swap(send0, "core")
    pair_recv = flip(pair, "z", 8, 1)
    dq_recv = [flip(d, "z", 8, QUAD[k]) for k, d in zip((1, 2, 3), dq_sends)]
    (grads,) = call(
        collect_kernel,
        [((slab + own, 2 * width), BF)],
        (keep0, recv, pair_recv, dq0, *dq_recv),
    )
    grads_other = swap(grads, "core")

    part = model // 8
    kv_own, *kv_sends, qo_keep, qo_send = call(
        functools.partial(weights_kernel, own),
        [((part, 2 * width), F32)]
        + [((part, 2 * width), BF)] * 3
        + [((2 * part, 2 * width), F32), ((2 * part, 2 * width), BF)],
        (xt, xt_other, grads, grads_other),
    )
    kv_x = [flip(kv_sends[k - 1], "dp", 4, k) for k in (2, 1, 3)]
    qo_b = flip(qo_send, "z", 8, 1)

    held, kv_own = lax.optimization_barrier((grads, kv_own))
    own_part, *sends = pl.pallas_call(
        inputs_kernel,
        out_shape=[jax.ShapeDtypeStruct((slab + own, width), F32)]
        + [jax.ShapeDtypeStruct((slab + own, width), BF)] * 3,
        in_specs=[SMEM, VMEM] + [pl.BlockSpec(memory_space=pltpu.HBM)] * 3,
        out_specs=[VMEM] * 4,
        scratch_shapes=[pltpu.VMEM((4, slab + own, width), F32)]
        + weights[:3]
        + [pltpu.SemaphoreType.DMA((6,))],
        compiler_params=pltpu.CompilerParams(vmem_limit_bytes=18 * 1024 * 1024),
        cost_estimate=pl.CostEstimate(
            flops=12_000_000_000, bytes_accessed=0, transcendentals=0
        ),
    )(where, held, wk_t, wv_t, wq_t)
    arrived = [flip(sends[k - 1], "head", 4, k) for k in (2, 1)]

    cut = part // 2
    kv_sum = kv_own + sum(k.astype(F32) for k in kv_x)
    kv_b = flip(kv_sum[cut:].astype(BF), "z", 8, 1)
    qo_sum = qo_keep + qo_b.astype(F32)
    qo_x = [flip(qo_sum[k * cut : (k + 1) * cut].astype(BF), "dp", 4, k) for k in (2, 1, 3)]
    kv_sum = kv_sum[:cut] + kv_b.astype(F32)
    qo_sum = qo_sum[:cut] + sum(q.astype(F32) for q in qo_x)
    total = jnp.concatenate([kv_sum, qo_sum], axis=1)
    total, sends[2], arrived = lax.optimization_barrier((total, sends[2], arrived))
    arrived.append(flip(sends[2], "head", 4, 3))
    low = total.astype(BF)
    over = [flip(low[k * inner : (k + 1) * inner], "z", 8, QUAD[k]) for k in (2, 1, 3)]
    total = total[:inner] + sum(p.astype(F32) for p in over)
    dframes = (own_part[:slab] + sum(p[:slab].astype(F32) for p in arrived)).astype(BF)
    dinput = (own_part[slab:] + sum(p[slab:].astype(F32) for p in arrived)).astype(BF)
    return (
        dinput[None],
        dframes[None],
        total[:, 2 * width : 3 * width],
        total[:, :width],
        total[:, width : 2 * width],
        total[:, 3 * width :].T,
    )


def solution(mesh):
    dp, tm, head = mesh.devices.shape
    fine = Mesh(mesh.devices.reshape(dp, tm // 2, 2, head), ("dp", "z", "core", "head"))
    tm = ("z", "core")
    placed = (
        P("dp", tm, None),
        P("dp", tm, None),
        P("dp", tm, None),
        P("dp"),
        P(None, "head"),
        P(None, "head"),
        P(None, "head"),
        P("head", None),
    )
    every = ("dp",) + tm
    return jax.shard_map(
        per_device,
        mesh=fine,
        in_specs=placed,
        out_specs=(
            P("dp", tm, "head"),
            P("dp", tm, "head"),
            P(every, "head"),
            P(every, "head"),
            P(every, "head"),
            P("head", every),
        ),
        check_vma=False,
    )
```
